32 devices in a mesh: ctx: 8 (over z, x), head: 4 (over y, core).
Axes of the slice: x: 2, y: 2, z: 4, core: 2. Of those that a mesh axis runs over, the one named last changes fastest.
Arguments:
- queries: bfloat16 [2048, 32, 128], P('ctx', 'head'), may hold values from -40 to 40
- keys: bfloat16 [2048, 8, 128], P('ctx', 'head'), may hold values from -40 to 40
- values: bfloat16 [2048, 8, 128], P('ctx', 'head'), may hold values from -6 to 6
- doc_ids: int32 [2048], P('ctx'), may hold values from 0 to 3, never falling along the last dimension, each value on 1 to 1024 neighbouring positions
Outputs:
- attended: bfloat16 [2048, 4096], P(('ctx', 'head'))
The draws below stay inside these ranges and needn't reach their ends.
Inputs may be any that keep to these rules, and one draw needn't show every extreme that they name: `doc_ids`: document numbers never fall along the sequence; each document has 1 to 1024 tokens and one has exactly 1024.
All inputs are finite; a program needn't handle non-finite values.
Results may differ from the reference program's by a relative error of at most 0.009.
Values may be sent and summed in bfloat16 or wider, within the bound.
A program may use at most 128 MiB of HBM per device.

```python
import math
import jax
import jax.numpy as jnp
import numpy as np
from jax import lax

QUERY_HEADS = 32
KEY_VALUE_HEADS = 8
HEAD_SIZE = 128
SEGS = 4
SEQUENCE_TOKENS = 2048


def draw_keys(key, part):
    starting_matrix = jax.random.truncated_normal(jax.random.fold_in(key, 2), -6.0, 6.0, (SEQUENCE_TOKENS, KEY_VALUE_HEADS, HEAD_SIZE), jnp.float32)
    return starting_matrix.astype(jnp.bfloat16)


def draw_queries(key, part):
    starting_matrix = jax.random.truncated_normal(jax.random.fold_in(key, 1), -6.0, 6.0, (SEQUENCE_TOKENS, QUERY_HEADS, HEAD_SIZE), jnp.float32)
    return starting_matrix.astype(jnp.bfloat16)


def steps_of(stream_key, extent, split, smallest, high):
    def one(position, shards_of):
        heights = jax.random.uniform(jax.random.fold_in(jax.random.fold_in(stream_key, 6), position), (shards_of,), jnp.float32, smallest / len(split), high / len(split))
        return jnp.repeat(jnp.exp(heights), extent[position] // shards_of).reshape((-1,) + (1,) * (len(extent) - position - 1))

    factor_of = one(*split[0])
    for cut in split[1:]:
        factor_of = factor_of * one(*cut)
    return factor_of


def profile(amount, total, bound, slope):
    loads = [(1 << 20) // math.isqrt(standing ** slope) + 1 for standing in range(2, amount + 1)]
    spare, holding = total - bound - (amount - 1), [1] * (amount - 1)
    while spare > 0:
        candidates = [i for i in range(amount - 1) if holding[i] < bound]
        whole, remaining = sum([loads[i] for i in candidates]), spare
        for i in candidates:
            addition = min(bound - holding[i], max(1, remaining * loads[i] // whole), spare)
            holding[i] = holding[i] + addition
            spare = spare - addition
    return np.array([bound] + holding)


def uneven(stream_key, amount, total, reach, lean):
    if amount == 2:
        one = jax.random.randint(stream_key, (), max(1, total - reach), min(reach, total - 1) + 1)
        return jnp.stack([one, total - one])
    lengths = jnp.asarray(profile(amount, total, reach, lean), jnp.int32)
    twos = (amount - 1) // 2
    giver, taker = lengths[1:1 + 2 * twos:2], lengths[2:2 + 2 * twos:2]
    room = jnp.minimum(giver - 1, reach - taker)
    passed = jax.random.randint(jax.random.fold_in(stream_key, 1), (twos,), 0, 1 << 20) % (room + 1)
    lengths = lengths.at[1:1 + 2 * twos:2].set(giver - passed).at[2:2 + 2 * twos:2].set(taker + passed)
    return lengths[jax.random.permutation(jax.random.fold_in(stream_key, 2), amount)]


def centred(own_key, extent, scale, most, shards=(), kind=jnp.bfloat16):
    entries = jax.random.normal(own_key, extent, jnp.float32) * scale
    if len(shards) > 0:
        entries = steps_of(own_key, extent, shards, -0.22, 0.18) * entries
    return jnp.clip(entries, min=-most, max=most).astype(kind)


def setup_inputs(seed: int = 0) -> dict:
    arg_keys = jax.random.split(jax.random.key(seed), 5)
    return {
        "queries": draw_queries(jax.random.fold_in(arg_keys[4], 71), 0),
        "keys": draw_keys(jax.random.fold_in(arg_keys[4], 71), 0),
        "values": centred(arg_keys[2], (SEQUENCE_TOKENS, KEY_VALUE_HEADS, HEAD_SIZE), 1.0, 6.0, ((0, 8), (1, 4))),
        "doc_ids": jnp.searchsorted(jnp.cumsum(uneven(arg_keys[3], SEGS, SEQUENCE_TOKENS, SEQUENCE_TOKENS // 2, 0)), jnp.arange(SEQUENCE_TOKENS), side="right").astype(jnp.int32),
    }


def reference(queries, keys, values, doc_ids):
    total_len, q_heads, head_dim = queries.shape
    kv_heads = keys.shape[1]
    group_size = q_heads // kv_heads
    block_rows = math.gcd(total_len, 1024)
    block_count = total_len // block_rows
    score_scale = head_dim ** -0.5

    def one_head(head_index):
        kv_index = head_index // group_size
        query_head = lax.dynamic_index_in_dim(queries, head_index, 1, keepdims=False).astype(jnp.float32)
        key_head = lax.dynamic_index_in_dim(keys, kv_index, 1, keepdims=False).astype(jnp.float32)
        value_head = lax.dynamic_index_in_dim(values, kv_index, 1, keepdims=False).astype(jnp.float32)
        key_pos = jnp.arange(total_len, dtype=jnp.int32)

        def one_block(block_index):
            first_row = (block_index * block_rows).astype(jnp.int32)
            query_block = lax.dynamic_slice_in_dim(query_head, first_row, block_rows, 0)
            query_pos = first_row + jnp.arange(block_rows, dtype=jnp.int32)
            query_ids = lax.dynamic_slice_in_dim(doc_ids, first_row, block_rows, 0)
            scores = jnp.dot(query_block, key_head.T, preferred_element_type=jnp.float32,
                             precision=lax.Precision.HIGHEST) * score_scale
            visible = (key_pos[None, :] <= query_pos[:, None]) & (doc_ids[None, :] == query_ids[:, None])
            masked = jnp.where(visible, scores, jnp.float32(-1e30))
            top_score = jnp.max(masked, axis=1, keepdims=True)
            expo = jnp.where(visible, jnp.exp(masked - top_score), jnp.float32(0.0))
            weights = expo / jnp.sum(expo, axis=1, keepdims=True)
            rounded = lax.optimization_barrier(weights.astype(jnp.bfloat16)).astype(jnp.float32)
            return jnp.dot(rounded, value_head, preferred_element_type=jnp.float32,
                           precision=lax.Precision.HIGHEST)

        blocks_out = lax.map(one_block, jnp.arange(block_count, dtype=jnp.int32))
        return blocks_out.reshape(total_len, head_dim)

    heads_out = lax.map(one_head, jnp.arange(q_heads, dtype=jnp.int32))
    joined = jnp.transpose(heads_out, (1, 0, 2)).reshape(total_len, q_heads * head_dim)
    return joined.astype(jnp.bfloat16)
```

```python
import functools
import math

import jax
import jax.numpy as jnp
from jax import lax
from jax.experimental import pallas as pl
from jax.experimental.pallas import tpu as pltpu
from jax.sharding import PartitionSpec as P

MESH = pl.DeviceIdType.MESH
HIDDEN = -1e30
ID_ROWS = 16


def inner_size(mesh):
    axes = list(mesh.axis_names)
    column = mesh.devices if axes.index("ctx") == 0 else mesh.devices.T
    places = [getattr(device, "coords", None) for device in column[:, 0]]
    count = len(places)
    if count < 2 or any(place is None for place in places):
        return 1
    moved = [i for i in range(len(places[0])) if places[0][i] != places[1][i]]
    if len(moved) != 1:
        return 1
    inner = len({place[moved[0]] for place in places})
    return inner if count % (2 * inner) == 0 else 1


def kernel(
    outer, inner, heads,
    q_ref, k_ref, v_ref, id_ref, out_ref,
    kv, qs, top, acc, done, id_col,
    along_send, across_send, block_recv, out_send, out_recv,
):
    reach = outer // 2
    q_heads, rows, size = qs.shape
    kv_heads = kv.shape[2] // 2
    group = q_heads // kv_heads
    out_rows = out_ref.shape[0]
    pieces = 2 * kv_heads
    factor = size ** -0.5 * math.log2(math.e)

    me = lax.axis_index("ctx")
    a, b = me // inner, me % inner
    place = lax.axis_index("head")
    has_prev, has_next = a > 0, a < outer - 1

    def span(p):
        return pl.ds(0, rows + ID_ROWS) if p == 0 else pl.ds(0, rows)

    barrier = pltpu.get_barrier_semaphore()

    def greet(device_id):
        pl.semaphore_signal(barrier, inc=1, device_id=device_id, device_id_type=MESH)

    @pl.when(has_prev)
    def _():
        greet({"ctx": me - inner})

    @pl.when(has_next)
    def _():
        greet({"ctx": me + inner})

    for step in range(1, inner):
        greet({"ctx": a * inner + (b + step) % inner})
    for step in range(1, heads):
        greet({"head": (place + step) % heads})

    def split_heads(ref, count, store):
        chunk = min(256, ref.shape[0])
        tokens = chunk // count
        row = lax.broadcasted_iota(jnp.int32, (chunk, chunk), 0)
        col = lax.broadcasted_iota(jnp.int32, (chunk, chunk), 1)
        order = jnp.where(col == (row % tokens) * count + row // tokens, 1.0, 0.0).astype(jnp.bfloat16)
        for i in range(ref.shape[0] // chunk):
            part = ref[i * chunk:(i + 1) * chunk, :]
            moved = jnp.dot(order, part, preferred_element_type=jnp.float32).astype(jnp.bfloat16)
            for h in range(count):
                store(h, pl.ds(i * tokens, tokens), moved[h * tokens:(h + 1) * tokens])

    def store_k(h, where, value):
        kv[0, b, 2 * h, where, :] = value

    def store_v(h, where, value):
        kv[0, b, 2 * h + 1, where, :] = value

    def store_q(h, where, value):
        qs[h, where, :] = value

    split_heads(k_ref, kv_heads, store_k)
    split_heads(v_ref, kv_heads, store_v)
    numbers = id_ref[...].astype(jnp.float32)
    line = lax.broadcasted_iota(jnp.int32, (ID_ROWS, size), 0)
    lines = jnp.zeros((ID_ROWS, size), jnp.float32)
    for i in range(rows // size):
        lines = jnp.where(line == i, numbers[i:i + 1, :], lines)
    kv[0, b, 0, rows:rows + ID_ROWS, :] = lines.astype(jnp.bfloat16)

    greeted = has_prev.astype(jnp.int32) + has_next.astype(jnp.int32) + (inner - 1) + (heads - 1)
    pl.semaphore_wait(barrier, greeted)

    def along(da, p):
        return pltpu.make_async_remote_copy(
            src_ref=kv.at[da, b, p, span(p)],
            dst_ref=kv.at[da + 1, b, p, span(p)],
            send_sem=along_send.at[da, p],
            recv_sem=block_recv.at[da + 1, b, p],
            device_id={"ctx": me + inner},
            device_id_type=MESH,
        )

    def across(da, p, to):
        return pltpu.make_async_remote_copy(
            src_ref=kv.at[da, b, p, span(p)],
            dst_ref=kv.at[da, b, p, span(p)],
            send_sem=across_send.at[da, to, p],
            recv_sem=block_recv.at[da, b, p],
            device_id={"ctx": a * inner + to},
            device_id_type=MESH,
        )

    def landed(da, at, p):
        return pltpu.make_async_remote_copy(
            src_ref=kv.at[da, at, p, span(p)],
            dst_ref=kv.at[da, at, p, span(p)],
            send_sem=along_send.at[0, p],
            recv_sem=block_recv.at[da, at, p],
            device_id={"ctx": me},
            device_id_type=MESH,
        )

    def needed(da, src, dst):
        if da == 0:
            return src < dst
        if da == reach:
            return src > dst
        return src != dst

    def spread(da, p, act):
        if da < reach:
            @pl.when(has_next)
            def _():
                act(along(da, p))
        for step in range(1, inner):
            to = (b + step) % inner

            @pl.when(needed(da, b, to))
            def _():
                act(across(da, p, to))

    for p in range(pieces):
        spread(0, p, lambda copy: copy.start())

    split_heads(q_ref, q_heads, store_q)

    row = lax.broadcasted_iota(jnp.int32, (rows, rows), 0)
    col = lax.broadcasted_iota(jnp.int32, (rows, rows), 1)

    def key_ids(da, at):
        held = kv[da, at, 0, rows:rows + ID_ROWS, :].astype(jnp.float32)
        return jnp.concatenate([held[i:i + 1, :] for i in range(rows // size)], axis=1)

    own_ids = key_ids(0, b)
    column = jnp.sum(jnp.where(row == col, own_ids, 0.0), axis=1, keepdims=True)
    id_col[...] = jnp.broadcast_to(column, id_col.shape)

    def wide(value, width):
        return jnp.concatenate([value] * (width // value.shape[1]), axis=1)

    def attend(da, at, g, first=False):
        same = wide(id_col[...], rows) == key_ids(da, at)
        if first:
            same = same & (col <= row)
        bias = jnp.where(same, 0.0, HIDDEN)
        keys = kv[da, at, 2 * g, :rows, :]
        values = kv[da, at, 2 * g + 1, :rows, :]
        values = jnp.concatenate([values, jnp.ones_like(values)], axis=1)
        for j in range(group):
            h = g * group + j
            scores = lax.dot_general(
                qs[h], keys, (((1,), (1,)), ((), ())), preferred_element_type=jnp.float32
            ) + bias
            highest = jnp.broadcast_to(jnp.max(scores, axis=1, keepdims=True), (rows, size))
            if not first:
                old = top[h]
                highest = jnp.maximum(old, highest)
            weights = jnp.exp2((scores - wide(highest, rows)) * factor).astype(jnp.bfloat16)
            product = jnp.dot(weights, values, preferred_element_type=jnp.float32)
            if not first:
                product = acc[h] * wide(jnp.exp2((old - highest) * factor), 2 * size) + product
            top[h] = highest
            acc[h] = product

    def pass_on(da, g):
        @pl.when(a >= da)
        def _():
            for p in (2 * g, 2 * g + 1):
                landed(da, b, p).wait_recv()
                spread(da, p, lambda copy: copy.start())

    def column_block(da, g):
        @pl.when(a >= da)
        def _():
            attend(da, b, g)

    def inner_blocks(da, g):
        if inner == 1:
            return

        def one(step, carry):
            at = (b + step) % inner

            @pl.when((a >= da) & needed(da, at, b))
            def _():
                for p in (2 * g, 2 * g + 1):
                    landed(da, at, p).wait_recv()
                attend(da, at, g)

            return carry

        lax.fori_loop(1, inner, one, 0)

    def give(h, to):
        return pltpu.make_async_remote_copy(
            src_ref=done.at[h, pl.ds(to * out_rows, out_rows)],
            dst_ref=out_ref.at[:, pl.ds(pl.multiple_of((place * q_heads + h) * size, size), size)],
            send_sem=out_send.at[h, to],
            recv_sem=out_recv.at[h, place],
            device_id={"head": to},
            device_id_type=MESH,
        )

    def taken(h, source):
        return pltpu.make_async_remote_copy(
            src_ref=done.at[h, pl.ds(0, out_rows)],
            dst_ref=out_ref.at[:, pl.ds(pl.multiple_of((source * q_heads + h) * size, size), size)],
            send_sem=out_send.at[h, source],
            recv_sem=out_recv.at[h, source],
            device_id={"head": source},
            device_id_type=MESH,
        )

    def finish(g):
        for j in range(group):
            h = g * group + j
            total = acc[h]
            done[h] = (total[:, :size] / total[:, size:]).astype(jnp.bfloat16)
            for step in range(1, heads):
                give(h, (place + step) % heads).start()
        for j in range(group):
            h = g * group + j
            out_ref[:, pl.ds(pl.multiple_of((place * q_heads + h) * size, size), size)] = done[
                h, pl.ds(pl.multiple_of(place * out_rows, out_rows), out_rows), :
            ]

    groups = range(kv_heads)
    for g in groups:
        attend(0, b, g, first=True)
    for da in range(1, reach + 1):
        if da < reach:
            for g in groups:
                pass_on(da, g)
                column_block(da, g)
                inner_blocks(da - 1, g)
        else:
            for g in groups:
                pass_on(da, g)
                if g > 0:
                    inner_blocks(da, g - 1)
                    finish(g - 1)
                else:
                    for other in groups:
                        inner_blocks(da - 1, other)
                column_block(da, g)
            inner_blocks(da, kv_heads - 1)
            finish(kv_heads - 1)

    for h in range(q_heads):
        for step in range(1, heads):
            taken(h, (place + step) % heads).wait_recv()
    for da in range(reach + 1):
        @pl.when(a >= da)
        def _():
            for p in range(pieces):
                spread(da, p, lambda copy: copy.wait_send())
    for h in range(q_heads):
        for step in range(1, heads):
            give(h, (place + step) % heads).wait_send()


def local(outer, inner, heads, queries, keys, values, doc_ids):
    rows, q_heads, size = queries.shape
    kv_heads = keys.shape[1]
    reach = outer // 2
    return pl.pallas_call(
        functools.partial(kernel, outer, inner, heads),
        out_shape=jax.ShapeDtypeStruct((rows // heads, heads * q_heads * size), jnp.bfloat16),
        in_specs=[pl.BlockSpec(memory_space=pltpu.VMEM)] * 4,
        out_specs=pl.BlockSpec(memory_space=pltpu.VMEM),
        scratch_shapes=[
            pltpu.VMEM((reach + 1, inner, 2 * kv_heads, rows + ID_ROWS, size), jnp.bfloat16),
            pltpu.VMEM((q_heads, rows, size), jnp.bfloat16),
            pltpu.VMEM((q_heads, rows, size), jnp.float32),
            pltpu.VMEM((q_heads, rows, 2 * size), jnp.float32),
            pltpu.VMEM((q_heads, rows, size), jnp.bfloat16),
            pltpu.VMEM((rows, size), jnp.float32),
            pltpu.SemaphoreType.DMA((reach, 2 * kv_heads)),
            pltpu.SemaphoreType.DMA((reach + 1, inner, 2 * kv_heads)),
            pltpu.SemaphoreType.DMA((reach + 1, inner, 2 * kv_heads)),
            pltpu.SemaphoreType.DMA((q_heads, heads)),
            pltpu.SemaphoreType.DMA((q_heads, heads)),
        ],
        compiler_params=pltpu.CompilerParams(
            collective_id=0, has_side_effects=True, vmem_limit_bytes=48 * 1024 * 1024
        ),
    )(
        queries.reshape(rows * q_heads, size),
        keys.reshape(rows * kv_heads, size),
        values.reshape(rows * kv_heads, size),
        doc_ids.reshape(rows // size, size),
    )


def solution(mesh):
    inner = inner_size(mesh)
    return jax.shard_map(
        functools.partial(local, mesh.shape["ctx"] // inner, inner, mesh.shape["head"]),
        mesh=mesh,
        in_specs=(P("ctx", "head", None), P("ctx", "head", None), P("ctx", "head", None), P("ctx")),
        out_specs=P(("ctx", "head"), None),
        check_vma=False,
    )
```

```python
import functools
import math

import jax
import jax.numpy as jnp
from jax import lax
from jax.experimental import pallas as pl
from jax.experimental.pallas import tpu as pltpu
from jax.sharding import PartitionSpec as P

MESH = pl.DeviceIdType.MESH
HIDDEN = -1e30
ID_ROWS = 16


def inner_size(mesh):
    axes = list(mesh.axis_names)
    column = mesh.devices if axes.index("ctx") == 0 else mesh.devices.T
    places = [getattr(device, "coords", None) for device in column[:, 0]]
    count = len(places)
    if count < 2 or any(place is None for place in places):
        return 1
    moved = [i for i in range(len(places[0])) if places[0][i] != places[1][i]]
    if len(moved) != 1:
        return 1
    inner = len({place[moved[0]] for place in places})
    return inner if count % (2 * inner) == 0 else 1


def kernel(
    outer, inner, heads,
    q_hbm, k_hbm, v_hbm, id_hbm, out_ref,
    q_ref, k_ref, v_ref, id_ref, loaded, kv, qs, top, acc, done, id_col,
    along_send, across_send, block_recv, out_send, out_recv,
):
    reach = outer // 2
    q_heads, rows, size = qs.shape
    kv_heads = kv.shape[2] // 2
    group = q_heads // kv_heads
    out_rows = out_ref.shape[0]
    pieces = 2 * kv_heads
    factor = size ** -0.5 * math.log2(math.e)

    me = lax.axis_index("ctx")
    a, b = me // inner, me % inner
    place = lax.axis_index("head")
    has_prev, has_next = a > 0, a < outer - 1

    def span(p):
        return pl.ds(0, rows + ID_ROWS) if p == 0 else pl.ds(0, rows)

    loads = [
        pltpu.make_async_copy(source, held, loaded.at[i])
        for i, (source, held) in enumerate(
            ((k_hbm, k_ref), (v_hbm, v_ref), (id_hbm, id_ref), (q_hbm, q_ref))
        )
    ]
    for load in loads:
        load.start()

    barrier = pltpu.get_barrier_semaphore()

    def greet(device_id):
        pl.semaphore_signal(barrier, inc=1, device_id=device_id, device_id_type=MESH)

    @pl.when(has_prev)
    def _():
        greet({"ctx": me - inner})

    @pl.when(has_next)
    def _():
        greet({"ctx": me + inner})

    for step in range(1, inner):
        greet({"ctx": a * inner + (b + step) % inner})
    for step in range(1, heads):
        greet({"head": (place + step) % heads})

    def split_heads(ref, count, store):
        chunk = min(256, ref.shape[0])
        tokens = chunk // count
        row = lax.broadcasted_iota(jnp.int32, (chunk, chunk), 0)
        col = lax.broadcasted_iota(jnp.int32, (chunk, chunk), 1)
        order = jnp.where(col == (row % tokens) * count + row // tokens, 1.0, 0.0).astype(jnp.bfloat16)
        for i in range(ref.shape[0] // chunk):
            part = ref[i * chunk:(i + 1) * chunk, :]
            moved = jnp.dot(order, part, preferred_element_type=jnp.float32).astype(jnp.bfloat16)
            for h in range(count):
                store(h, pl.ds(i * tokens, tokens), moved[h * tokens:(h + 1) * tokens])

    def store_k(h, where, value):
        kv[0, b, 2 * h, where, :] = value

    def store_v(h, where, value):
        kv[0, b, 2 * h + 1, where, :] = value

    def store_q(h, where, value):
        qs[h, where, :] = value

    loads[0].wait()
    split_heads(k_ref, kv_heads, store_k)
    loads[1].wait()
    split_heads(v_ref, kv_heads, store_v)
    loads[2].wait()
    numbers = id_ref[...].astype(jnp.float32)
    line = lax.broadcasted_iota(jnp.int32, (ID_ROWS, size), 0)
    lines = jnp.zeros((ID_ROWS, size), jnp.float32)
    for i in range(rows // size):
        lines = jnp.where(line == i, numbers[i:i + 1, :], lines)
    kv[0, b, 0, rows:rows + ID_ROWS, :] = lines.astype(jnp.bfloat16)

    greeted = has_prev.astype(jnp.int32) + has_next.astype(jnp.int32) + (inner - 1) + (heads - 1)
    pl.semaphore_wait(barrier, greeted)

    def along(da, p):
        return pltpu.make_async_remote_copy(
            src_ref=kv.at[da, b, p, span(p)],
            dst_ref=kv.at[da + 1, b, p, span(p)],
            send_sem=along_send.at[da, p],
            recv_sem=block_recv.at[da + 1, b, p],
            device_id={"ctx": me + inner},
            device_id_type=MESH,
        )

    def across(da, p, to):
        return pltpu.make_async_remote_copy(
            src_ref=kv.at[da, b, p, span(p)],
            dst_ref=kv.at[da, b, p, span(p)],
            send_sem=across_send.at[da, to, p],
            recv_sem=block_recv.at[da, b, p],
            device_id={"ctx": a * inner + to},
            device_id_type=MESH,
        )

    def landed(da, at, p):
        return pltpu.make_async_remote_copy(
            src_ref=kv.at[da, at, p, span(p)],
            dst_ref=kv.at[da, at, p, span(p)],
            send_sem=along_send.at[0, p],
            recv_sem=block_recv.at[da, at, p],
            device_id={"ctx": me},
            device_id_type=MESH,
        )

    def needed(da, src, dst):
        if da == 0:
            return src < dst
        if da == reach:
            return src > dst
        return src != dst

    def spread(da, p, act):
        if da < reach:
            @pl.when(has_next)
            def _():
                act(along(da, p))
        for step in range(1, inner):
            to = (b + step) % inner

            @pl.when(needed(da, b, to))
            def _():
                act(across(da, p, to))

    for p in range(pieces):
        spread(0, p, lambda copy: copy.start())

    loads[3].wait()
    split_heads(q_ref, q_heads, store_q)

    row = lax.broadcasted_iota(jnp.int32, (rows, rows), 0)
    col = lax.broadcasted_iota(jnp.int32, (rows, rows), 1)

    def key_ids(da, at):
        held = kv[da, at, 0, rows:rows + ID_ROWS, :].astype(jnp.float32)
        return jnp.concatenate([held[i:i + 1, :] for i in range(rows // size)], axis=1)

    own_ids = key_ids(0, b)
    column = jnp.sum(jnp.where(row == col, own_ids, 0.0), axis=1, keepdims=True)
    id_col[...] = jnp.broadcast_to(column, id_col.shape)

    def wide(value, width):
        return jnp.concatenate([value] * (width // value.shape[1]), axis=1)

    def attend(da, at, g, first=False):
        same = wide(id_col[...], rows) == key_ids(da, at)
        if first:
            same = same & (col <= row)
        bias = jnp.where(same, 0.0, HIDDEN)
        keys = kv[da, at, 2 * g, :rows, :]
        values = kv[da, at, 2 * g + 1, :rows, :]
        values = jnp.concatenate([values, jnp.ones_like(values)], axis=1)
        for j in range(group):
            h = g * group + j
            scores = lax.dot_general(
                qs[h], keys, (((1,), (1,)), ((), ())), preferred_element_type=jnp.float32
            ) + bias
            highest = jnp.broadcast_to(jnp.max(scores, axis=1, keepdims=True), (rows, size))
            if not first:
                old = top[h]
                highest = jnp.maximum(old, highest)
            weights = jnp.exp2((scores - wide(highest, rows)) * factor).astype(jnp.bfloat16)
            product = jnp.dot(weights, values, preferred_element_type=jnp.float32)
            if not first:
                product = acc[h] * wide(jnp.exp2((old - highest) * factor), 2 * size) + product
            top[h] = highest
            acc[h] = product

    def pass_on(da, *which):
        @pl.when(a >= da)
        def _():
            for p in which:
                landed(da, b, p).wait_recv()
                spread(da, p, lambda copy: copy.start())

    def column_block(da, g):
        @pl.when(a >= da)
        def _():
            attend(da, b, g)

    def inner_blocks(da, g):
        if inner == 1:
            return

        def one(step, carry):
            at = (b + step) % inner

            @pl.when((a >= da) & needed(da, at, b))
            def _():
                for p in (2 * g, 2 * g + 1):
                    landed(da, at, p).wait_recv()
                attend(da, at, g)

            return carry

        lax.fori_loop(1, inner, one, 0)

    def give(h, to):
        return pltpu.make_async_remote_copy(
            src_ref=done.at[h, pl.ds(to * out_rows, out_rows)],
            dst_ref=out_ref.at[:, pl.ds(pl.multiple_of((place * q_heads + h) * size, size), size)],
            send_sem=out_send.at[h, to],
            recv_sem=out_recv.at[h, place],
            device_id={"head": to},
            device_id_type=MESH,
        )

    def taken(h, source):
        return pltpu.make_async_remote_copy(
            src_ref=done.at[h, pl.ds(0, out_rows)],
            dst_ref=out_ref.at[:, pl.ds(pl.multiple_of((source * q_heads + h) * size, size), size)],
            send_sem=out_send.at[h, source],
            recv_sem=out_recv.at[h, source],
            device_id={"head": source},
            device_id_type=MESH,
        )

    def finish(g):
        for j in range(group):
            h = g * group + j
            total = acc[h]
            done[h] = (total[:, :size] / total[:, size:]).astype(jnp.bfloat16)
            for step in range(1, heads):
                give(h, (place + step) % heads).start()
        for j in range(group):
            h = g * group + j
            out_ref[:, pl.ds(pl.multiple_of((place * q_heads + h) * size, size), size)] = done[
                h, pl.ds(pl.multiple_of(place * out_rows, out_rows), out_rows), :
            ]

    groups = range(kv_heads)
    for g in groups:
        attend(0, b, g, first=True)
    for da in range(1, reach):
        pass_on(da, 0, 1)
        for g in groups:
            column_block(da, g)
            if g + 1 < kv_heads:
                pass_on(da, 2 * g + 2, 2 * g + 3)
            inner_blocks(da - 1, g)
    for g in groups:
        pass_on(reach, 2 * g)
        inner_blocks(reach - 1, g)
        pass_on(reach, 2 * g + 1)
        if g > 0:
            inner_blocks(reach, g - 1)
            finish(g - 1)
        column_block(reach, g)
    inner_blocks(reach, kv_heads - 1)
    finish(kv_heads - 1)

    for h in range(q_heads):
        for step in range(1, heads):
            taken(h, (place + step) % heads).wait_recv()
    for da in range(reach + 1):
        @pl.when(a >= da)
        def _():
            for p in range(pieces):
                spread(da, p, lambda copy: copy.wait_send())
    for h in range(q_heads):
        for step in range(1, heads):
            give(h, (place + step) % heads).wait_send()


def in_hbm(array):
    return pltpu.with_memory_space_constraint(array, pltpu.HBM)


def local(outer, inner, heads, queries, keys, values, doc_ids):
    rows, q_heads, size = queries.shape
    kv_heads = keys.shape[1]
    reach = outer // 2
    return pl.pallas_call(
        functools.partial(kernel, outer, inner, heads),
        out_shape=jax.ShapeDtypeStruct((rows // heads, heads * q_heads * size), jnp.bfloat16),
        in_specs=[pl.BlockSpec(memory_space=pltpu.HBM)] * 4,
        out_specs=pl.BlockSpec(memory_space=pltpu.VMEM),
        scratch_shapes=[
            pltpu.VMEM((rows * q_heads, size), jnp.bfloat16),
            pltpu.VMEM((rows * kv_heads, size), jnp.bfloat16),
            pltpu.VMEM((rows * kv_heads, size), jnp.bfloat16),
            pltpu.VMEM((rows // size, size), jnp.int32),
            pltpu.SemaphoreType.DMA((4,)),
            pltpu.VMEM((reach + 1, inner, 2 * kv_heads, rows + ID_ROWS, size), jnp.bfloat16),
            pltpu.VMEM((q_heads, rows, size), jnp.bfloat16),
            pltpu.VMEM((q_heads, rows, size), jnp.float32),
            pltpu.VMEM((q_heads, rows, 2 * size), jnp.float32),
            pltpu.VMEM((q_heads, rows, size), jnp.bfloat16),
            pltpu.VMEM((rows, size), jnp.float32),
            pltpu.SemaphoreType.DMA((reach, 2 * kv_heads)),
            pltpu.SemaphoreType.DMA((reach + 1, inner, 2 * kv_heads)),
            pltpu.SemaphoreType.DMA((reach + 1, inner, 2 * kv_heads)),
            pltpu.SemaphoreType.DMA((q_heads, heads)),
            pltpu.SemaphoreType.DMA((q_heads, heads)),
        ],
        compiler_params=pltpu.CompilerParams(
            collective_id=0, has_side_effects=True, vmem_limit_bytes=48 * 1024 * 1024
        ),
    )(
        in_hbm(queries.reshape(rows * q_heads, size)),
        in_hbm(keys.reshape(rows * kv_heads, size)),
        in_hbm(values.reshape(rows * kv_heads, size)),
        in_hbm(doc_ids.reshape(rows // size, size)),
    )


def solution(mesh):
    inner = inner_size(mesh)
    return jax.shard_map(
        functools.partial(local, mesh.shape["ctx"] // inner, inner, mesh.shape["head"]),
        mesh=mesh,
        in_specs=(P("ctx", "head", None), P("ctx", "head", None), P("ctx", "head", None), P("ctx")),
        out_specs=P(("ctx", "head"), None),
        check_vma=False,
    )
```

```python
import functools
import math

import jax
import jax.numpy as jnp
from jax import lax
from jax.experimental import pallas as pl
from jax.experimental.pallas import tpu as pltpu
from jax.sharding import PartitionSpec as P

MESH = pl.DeviceIdType.MESH
HIDDEN = -1e30
ID_ROWS = 16


def inner_size(mesh):
    axes = list(mesh.axis_names)
    column = mesh.devices if axes.index("ctx") == 0 else mesh.devices.T
    places = [getattr(device, "coords", None) for device in column[:, 0]]
    count = len(places)
    if count < 2 or any(place is None for place in places):
        return 1
    moved = [i for i in range(len(places[0])) if places[0][i] != places[1][i]]
    if len(moved) != 1:
        return 1
    inner = len({place[moved[0]] for place in places})
    return inner if count % (2 * inner) == 0 else 1


def kernel(
    outer, inner, heads,
    q_hbm, k_hbm, v_hbm, id_hbm, out_ref,
    q_ref, k_ref, v_ref, id_ref, loaded, kv, qs, top, acc, done, id_col,
    along_send, across_send, block_recv, out_send, out_recv,
):
    reach = outer // 2
    q_heads, rows, size = qs.shape
    kv_heads = kv.shape[2] // 2
    group = q_heads // kv_heads
    out_rows = out_ref.shape[0]
    pieces = 2 * kv_heads
    factor = size ** -0.5 * math.log2(math.e)

    me = lax.axis_index("ctx")
    a, b = me // inner, me % inner
    place = lax.axis_index("head")
    has_prev, has_next = a > 0, a < outer - 1

    def span(p):
        return pl.ds(0, rows + ID_ROWS) if p == 0 else pl.ds(0, rows)

    loads = [
        pltpu.make_async_copy(source, held, loaded.at[i])
        for i, (source, held) in enumerate(
            ((k_hbm, k_ref), (v_hbm, v_ref), (id_hbm, id_ref), (q_hbm, q_ref))
        )
    ]
    for load in loads:
        load.start()

    barrier = pltpu.get_barrier_semaphore()

    def greet(device_id):
        pl.semaphore_signal(barrier, inc=1, device_id=device_id, device_id_type=MESH)

    @pl.when(has_prev)
    def _():
        greet({"ctx": me - inner})

    @pl.when(has_next)
    def _():
        greet({"ctx": me + inner})

    for step in range(1, inner):
        greet({"ctx": a * inner + (b + step) % inner})
    for step in range(1, heads):
        greet({"head": (place + step) % heads})

    def split_heads(ref, count, store):
        chunk = min(256, ref.shape[0])
        tokens = chunk // count
        row = lax.broadcasted_iota(jnp.int32, (chunk, chunk), 0)
        col = lax.broadcasted_iota(jnp.int32, (chunk, chunk), 1)
        order = jnp.where(col == (row % tokens) * count + row // tokens, 1.0, 0.0).astype(jnp.bfloat16)
        for i in range(ref.shape[0] // chunk):
            part = ref[i * chunk:(i + 1) * chunk, :]
            moved = jnp.dot(order, part, preferred_element_type=jnp.float32).astype(jnp.bfloat16)
            for h in range(count):
                store(h, pl.ds(i * tokens, tokens), moved[h * tokens:(h + 1) * tokens])

    def store_k(h, where, value):
        kv[0, b, 2 * h, where, :] = value

    def store_v(h, where, value):
        kv[0, b, 2 * h + 1, where, :] = value

    def store_q(h, where, value):
        qs[h, where, :] = value

    loads[0].wait()
    split_heads(k_ref, kv_heads, store_k)
    loads[1].wait()
    split_heads(v_ref, kv_heads, store_v)
    loads[2].wait()
    numbers = id_ref[...].astype(jnp.float32)
    line = lax.broadcasted_iota(jnp.int32, (ID_ROWS, size), 0)
    lines = jnp.zeros((ID_ROWS, size), jnp.float32)
    for i in range(rows // size):
        lines = jnp.where(line == i, numbers[i:i + 1, :], lines)
    kv[0, b, 0, rows:rows + ID_ROWS, :] = lines.astype(jnp.bfloat16)

    greeted = has_prev.astype(jnp.int32) + has_next.astype(jnp.int32) + (inner - 1) + (heads - 1)
    pl.semaphore_wait(barrier, greeted)

    def along(da, p):
        return pltpu.make_async_remote_copy(
            src_ref=kv.at[da, b, p, span(p)],
            dst_ref=kv.at[da + 1, b, p, span(p)],
            send_sem=along_send.at[da, p],
            recv_sem=block_recv.at[da + 1, b, p],
            device_id={"ctx": me + inner},
            device_id_type=MESH,
        )

    def across(da, p, to):
        return pltpu.make_async_remote_copy(
            src_ref=kv.at[da, b, p, span(p)],
            dst_ref=kv.at[da, b, p, span(p)],
            send_sem=across_send.at[da, to, p],
            recv_sem=block_recv.at[da, b, p],
            device_id={"ctx": a * inner + to},
            device_id_type=MESH,
        )

    def landed(da, at, p):
        return pltpu.make_async_remote_copy(
            src_ref=kv.at[da, at, p, span(p)],
            dst_ref=kv.at[da, at, p, span(p)],
            send_sem=along_send.at[0, p],
            recv_sem=block_recv.at[da, at, p],
            device_id={"ctx": me},
            device_id_type=MESH,
        )

    def needed(da, src, dst):
        if da == 0:
            return src < dst
        if da == reach:
            return src > dst
        return src != dst

    def spread(da, p, act):
        if da < reach:
            @pl.when(has_next)
            def _():
                act(along(da, p))
        for step in range(1, inner):
            to = (b + step) % inner

            @pl.when(needed(da, b, to))
            def _():
                act(across(da, p, to))

    for p in range(pieces):
        spread(0, p, lambda copy: copy.start())

    loads[3].wait()
    split_heads(q_ref, q_heads, store_q)

    row = lax.broadcasted_iota(jnp.int32, (rows, rows), 0)
    col = lax.broadcasted_iota(jnp.int32, (rows, rows), 1)

    def key_ids(da, at):
        held = kv[da, at, 0, rows:rows + ID_ROWS, :].astype(jnp.float32)
        return jnp.concatenate([held[i:i + 1, :] for i in range(rows // size)], axis=1)

    own_ids = key_ids(0, b)
    column = jnp.sum(jnp.where(row == col, own_ids, 0.0), axis=1, keepdims=True)
    id_col[...] = jnp.broadcast_to(column, id_col.shape)

    def wide(value, width):
        return jnp.concatenate([value] * (width // value.shape[1]), axis=1)

    def attend(da, at, g, first=False):
        same = wide(id_col[...], rows) == key_ids(da, at)
        if first:
            same = same & (col <= row)
        bias = jnp.where(same, 0.0, HIDDEN)
        keys = kv[da, at, 2 * g, :rows, :]
        values = kv[da, at, 2 * g + 1, :rows, :]
        values = jnp.concatenate([values, jnp.ones_like(values)], axis=1)
        for j in range(group):
            h = g * group + j
            scores = lax.dot_general(
                qs[h], keys, (((1,), (1,)), ((), ())), preferred_element_type=jnp.float32
            ) + bias
            highest = jnp.broadcast_to(jnp.max(scores, axis=1, keepdims=True), (rows, size))
            if not first:
                old = top[h]
                highest = jnp.maximum(old, highest)
            weights = jnp.exp2((scores - wide(highest, rows)) * factor).astype(jnp.bfloat16)
            product = jnp.dot(weights, values, preferred_element_type=jnp.float32)
            if not first:
                product = acc[h] * wide(jnp.exp2((old - highest) * factor), 2 * size) + product
            top[h] = highest
            acc[h] = product

    def pass_on(da, *which):
        @pl.when(a >= da)
        def _():
            for p in which:
                landed(da, b, p).wait_recv()
                spread(da, p, lambda copy: copy.start())

    def column_block(da, g):
        @pl.when(a >= da)
        def _():
            attend(da, b, g)

    def inner_blocks(da, g):
        if inner == 1:
            return

        def one(step, carry):
            at = (b + step) % inner

            @pl.when((a >= da) & needed(da, at, b))
            def _():
                for p in (2 * g, 2 * g + 1):
                    landed(da, at, p).wait_recv()
                attend(da, at, g)

            return carry

        lax.fori_loop(1, inner, one, 0)

    def give(h, to):
        return pltpu.make_async_remote_copy(
            src_ref=done.at[h, pl.ds(to * out_rows, out_rows)],
            dst_ref=out_ref.at[:, pl.ds(pl.multiple_of((place * q_heads + h) * size, size), size)],
            send_sem=out_send.at[h, to],
            recv_sem=out_recv.at[h, place],
            device_id={"head": to},
            device_id_type=MESH,
        )

    def taken(h, source):
        return pltpu.make_async_remote_copy(
            src_ref=done.at[h, pl.ds(0, out_rows)],
            dst_ref=out_ref.at[:, pl.ds(pl.multiple_of((source * q_heads + h) * size, size), size)],
            send_sem=out_send.at[h, source],
            recv_sem=out_recv.at[h, source],
            device_id={"head": source},
            device_id_type=MESH,
        )

    def finish(g):
        for j in range(group):
            h = g * group + j
            total = acc[h]
            done[h] = (total[:, :size] / total[:, size:]).astype(jnp.bfloat16)
            for step in range(1, heads):
                give(h, (place + step) % heads).start()
        for j in range(group):
            h = g * group + j
            out_ref[:, pl.ds(pl.multiple_of((place * q_heads + h) * size, size), size)] = done[
                h, pl.ds(pl.multiple_of(place * out_rows, out_rows), out_rows), :
            ]

    groups = range(kv_heads)
    for g in groups:
        attend(0, b, g, first=True)
    for da in range(1, reach):
        pass_on(da, 0, 1)
        for g in groups:
            column_block(da, g)
            if g + 1 < kv_heads:
                inner_blocks(da - 1, g)
                pass_on(da, 2 * g + 2, 2 * g + 3)
            else:
                inner_blocks(da - 1, g)

    @pl.when(b > 0)
    def _():
        pass_on(reach, 0, 1)
        for g in groups:
            column_block(reach, g)
            if g + 1 < kv_heads:
                pass_on(reach, 2 * g + 2)
            inner_blocks(reach - 1, g)
            if g + 1 < kv_heads:
                pass_on(reach, 2 * g + 3)
            inner_blocks(reach, g)
            finish(g)

    @pl.when(b == 0)
    def _():
        for g in groups:
            inner_blocks(reach - 1, g)
        for g in groups:
            pass_on(reach, 2 * g, 2 * g + 1)
            column_block(reach, g)
            inner_blocks(reach, g)
            finish(g)

    for h in range(q_heads):
        for step in range(1, heads):
            taken(h, (place + step) % heads).wait_recv()
    for da in range(reach + 1):
        @pl.when(a >= da)
        def _():
            for p in range(pieces):
                spread(da, p, lambda copy: copy.wait_send())
    for h in range(q_heads):
        for step in range(1, heads):
            give(h, (place + step) % heads).wait_send()


def in_hbm(array):
    return pltpu.with_memory_space_constraint(array, pltpu.HBM)


def local(outer, inner, heads, queries, keys, values, doc_ids):
    rows, q_heads, size = queries.shape
    kv_heads = keys.shape[1]
    reach = outer // 2
    return pl.pallas_call(
        functools.partial(kernel, outer, inner, heads),
        out_shape=jax.ShapeDtypeStruct((rows // heads, heads * q_heads * size), jnp.bfloat16),
        in_specs=[pl.BlockSpec(memory_space=pltpu.HBM)] * 4,
        out_specs=pl.BlockSpec(memory_space=pltpu.VMEM),
        scratch_shapes=[
            pltpu.VMEM((rows * q_heads, size), jnp.bfloat16),
            pltpu.VMEM((rows * kv_heads, size), jnp.bfloat16),
            pltpu.VMEM((rows * kv_heads, size), jnp.bfloat16),
            pltpu.VMEM((rows // size, size), jnp.int32),
            pltpu.SemaphoreType.DMA((4,)),
            pltpu.VMEM((reach + 1, inner, 2 * kv_heads, rows + ID_ROWS, size), jnp.bfloat16),
            pltpu.VMEM((q_heads, rows, size), jnp.bfloat16),
            pltpu.VMEM((q_heads, rows, size), jnp.float32),
            pltpu.VMEM((q_heads, rows, 2 * size), jnp.float32),
            pltpu.VMEM((q_heads, rows, size), jnp.bfloat16),
            pltpu.VMEM((rows, size), jnp.float32),
            pltpu.SemaphoreType.DMA((reach, 2 * kv_heads)),
            pltpu.SemaphoreType.DMA((reach + 1, inner, 2 * kv_heads)),
            pltpu.SemaphoreType.DMA((reach + 1, inner, 2 * kv_heads)),
            pltpu.SemaphoreType.DMA((q_heads, heads)),
            pltpu.SemaphoreType.DMA((q_heads, heads)),
        ],
        compiler_params=pltpu.CompilerParams(
            collective_id=0, has_side_effects=True, vmem_limit_bytes=48 * 1024 * 1024
        ),
    )(
        in_hbm(queries.reshape(rows * q_heads, size)),
        in_hbm(keys.reshape(rows * kv_heads, size)),
        in_hbm(values.reshape(rows * kv_heads, size)),
        in_hbm(doc_ids.reshape(rows // size, size)),
    )


def solution(mesh):
    inner = inner_size(mesh)
    return jax.shard_map(
        functools.partial(local, mesh.shape["ctx"] // inner, inner, mesh.shape["head"]),
        mesh=mesh,
        in_specs=(P("ctx", "head", None), P("ctx", "head", None), P("ctx", "head", None), P("ctx")),
        out_specs=P(("ctx", "head"), None),
        check_vma=False,
    )
```

```python
import functools
import math

import jax
import jax.numpy as jnp
from jax import lax
from jax.experimental import pallas as pl
from jax.experimental.pallas import tpu as pltpu
from jax.sharding import PartitionSpec as P

MESH = pl.DeviceIdType.MESH
HIDDEN = -1e30
ID_ROWS = 16


def inner_size(mesh):
    axes = list(mesh.axis_names)
    column = mesh.devices if axes.index("ctx") == 0 else mesh.devices.T
    places = [getattr(device, "coords", None) for device in column[:, 0]]
    count = len(places)
    if count < 2 or any(place is None for place in places):
        return 1
    moved = [i for i in range(len(places[0])) if places[0][i] != places[1][i]]
    if len(moved) != 1:
        return 1
    inner = len({place[moved[0]] for place in places})
    return inner if count % (2 * inner) == 0 else 1


def kernel(
    outer, inner, heads,
    q_hbm, k_hbm, v_hbm, id_hbm, out_ref,
    q_ref, k_ref, v_ref, id_ref, loaded, kv, qs, top, acc, probs, done, id_col,
    along_send, across_send, direct_send, block_recv, out_send, out_recv,
):
    reach = outer // 2
    q_heads, rows, size = qs.shape
    kv_heads = kv.shape[2] // 2
    group = q_heads // kv_heads
    out_rows = out_ref.shape[0]
    pieces = 2 * kv_heads
    factor = size ** -0.5 * math.log2(math.e)

    me = lax.axis_index("ctx")
    a, b = me // inner, me % inner
    place = lax.axis_index("head")
    has_prev, has_next = a > 0, a < outer - 1

    def span(p):
        return pl.ds(0, rows + ID_ROWS) if p == 0 else pl.ds(0, rows)

    loads = [
        pltpu.make_async_copy(source, held, loaded.at[i])
        for i, (source, held) in enumerate(
            ((k_hbm, k_ref), (v_hbm, v_ref), (id_hbm, id_ref), (q_hbm, q_ref))
        )
    ]
    for load in loads:
        load.start()

    barrier = pltpu.get_barrier_semaphore()

    def greet(device_id):
        pl.semaphore_signal(barrier, inc=1, device_id=device_id, device_id_type=MESH)

    @pl.when(has_prev)
    def _():
        greet({"ctx": me - inner})

    @pl.when(has_next)
    def _():
        greet({"ctx": me + inner})

    for step in range(1, inner):
        greet({"ctx": a * inner + (b + step) % inner})
    for step in range(1, heads):
        greet({"head": (place + step) % heads})

    for step in range(1, inner):
        @pl.when(has_next & (step <= b))
        def _():
            greet({"ctx": me + inner - step})

        @pl.when(has_prev & (b + step < inner))
        def _():
            greet({"ctx": me - inner + step})

    def split_heads(ref, count, store):
        chunk = min(256, ref.shape[0])
        tokens = chunk // count
        row = lax.broadcasted_iota(jnp.int32, (chunk, chunk), 0)
        col = lax.broadcasted_iota(jnp.int32, (chunk, chunk), 1)
        order = jnp.where(col == (row % tokens) * count + row // tokens, 1.0, 0.0).astype(jnp.bfloat16)
        for i in range(ref.shape[0] // chunk):
            part = ref[i * chunk:(i + 1) * chunk, :]
            moved = jnp.dot(order, part, preferred_element_type=jnp.float32).astype(jnp.bfloat16)
            for h in range(count):
                store(h, pl.ds(i * tokens, tokens), moved[h * tokens:(h + 1) * tokens])

    def store_k(h, where, value):
        kv[0, b, 2 * h, where, :] = value

    def store_v(h, where, value):
        kv[0, b, 2 * h + 1, where, :] = value

    def store_q(h, where, value):
        qs[h, where, :] = value

    loads[0].wait()
    split_heads(k_ref, kv_heads, store_k)
    loads[1].wait()
    split_heads(v_ref, kv_heads, store_v)
    loads[2].wait()
    numbers = id_ref[...].astype(jnp.float32)
    line = lax.broadcasted_iota(jnp.int32, (ID_ROWS, size), 0)
    lines = jnp.zeros((ID_ROWS, size), jnp.float32)
    for i in range(rows // size):
        lines = jnp.where(line == i, numbers[i:i + 1, :], lines)
    kv[0, b, 0, rows:rows + ID_ROWS, :] = lines.astype(jnp.bfloat16)

    up, down = has_next.astype(jnp.int32), has_prev.astype(jnp.int32)
    greeted = up * (1 + b) + down * (inner - b) + (inner - 1) + (heads - 1)
    pl.semaphore_wait(barrier, greeted)

    def along(da, p):
        return pltpu.make_async_remote_copy(
            src_ref=kv.at[da, b, p, span(p)],
            dst_ref=kv.at[da + 1, b, p, span(p)],
            send_sem=along_send.at[da, p],
            recv_sem=block_recv.at[da + 1, b, p],
            device_id={"ctx": me + inner},
            device_id_type=MESH,
        )

    def across(da, p, to):
        return pltpu.make_async_remote_copy(
            src_ref=kv.at[da, b, p, span(p)],
            dst_ref=kv.at[da, b, p, span(p)],
            send_sem=across_send.at[da, to, p],
            recv_sem=block_recv.at[da, b, p],
            device_id={"ctx": a * inner + to},
            device_id_type=MESH,
        )

    def direct(step):
        p = pieces - 1
        return pltpu.make_async_remote_copy(
            src_ref=kv.at[reach - 1, b, p, span(p)],
            dst_ref=kv.at[reach, b, p, span(p)],
            send_sem=direct_send.at[step],
            recv_sem=block_recv.at[reach, b, p],
            device_id={"ctx": me + inner - step},
            device_id_type=MESH,
        )

    def landed(da, at, p):
        return pltpu.make_async_remote_copy(
            src_ref=kv.at[da, at, p, span(p)],
            dst_ref=kv.at[da, at, p, span(p)],
            send_sem=along_send.at[0, p],
            recv_sem=block_recv.at[da, at, p],
            device_id={"ctx": me},
            device_id_type=MESH,
        )

    def needed(da, src, dst):
        if da == 0:
            return src < dst
        if da == reach:
            return src > dst
        return src != dst

    def spread(da, p, act):
        if da < reach:
            @pl.when(has_next)
            def _():
                act(along(da, p))
        for step in range(1, inner):
            to = (b + step) % inner
            if p == pieces - 1 and da == reach - 1:
                @pl.when(has_next & (step <= b))
                def _():
                    act(direct(step))
            if p == pieces - 1 and da == reach:
                continue

            @pl.when(needed(da, b, to))
            def _():
                act(across(da, p, to))

    for p in range(pieces):
        spread(0, p, lambda copy: copy.start())

    loads[3].wait()
    split_heads(q_ref, q_heads, store_q)

    row = lax.broadcasted_iota(jnp.int32, (rows, rows), 0)
    col = lax.broadcasted_iota(jnp.int32, (rows, rows), 1)

    def key_ids(da, at):
        held = kv[da, at, 0, rows:rows + ID_ROWS, :].astype(jnp.float32)
        return jnp.concatenate([held[i:i + 1, :] for i in range(rows // size)], axis=1)

    own_ids = key_ids(0, b)
    column = jnp.sum(jnp.where(row == col, own_ids, 0.0), axis=1, keepdims=True)
    id_col[...] = jnp.broadcast_to(column, id_col.shape)

    def wide(value, width):
        return jnp.concatenate([value] * (width // value.shape[1]), axis=1)

    def attend(da, at, g, first=False):
        same = wide(id_col[...], rows) == key_ids(da, at)
        if first:
            same = same & (col <= row)
        bias = jnp.where(same, 0.0, HIDDEN)
        keys = kv[da, at, 2 * g, :rows, :]
        values = kv[da, at, 2 * g + 1, :rows, :]
        values = jnp.concatenate([values, jnp.ones_like(values)], axis=1)
        for j in range(group):
            h = g * group + j
            scores = lax.dot_general(
                qs[h], keys, (((1,), (1,)), ((), ())), preferred_element_type=jnp.float32
            ) + bias
            highest = jnp.broadcast_to(jnp.max(scores, axis=1, keepdims=True), (rows, size))
            if not first:
                old = top[h]
                highest = jnp.maximum(old, highest)
            weights = jnp.exp2((scores - wide(highest, rows)) * factor).astype(jnp.bfloat16)
            product = jnp.dot(weights, values, preferred_element_type=jnp.float32)
            if not first:
                product = acc[h] * wide(jnp.exp2((old - highest) * factor), 2 * size) + product
            top[h] = highest
            acc[h] = product

    def attend_last(da, at, g):
        landed(da, at, 2 * g).wait_recv()
        bias = jnp.where(wide(id_col[...], rows) == key_ids(da, at), 0.0, HIDDEN)
        keys = kv[da, at, 2 * g, :rows, :]
        for j in range(group):
            h = g * group + j
            scores = lax.dot_general(
                qs[h], keys, (((1,), (1,)), ((), ())), preferred_element_type=jnp.float32
            ) + bias
            old = top[h]
            highest = jnp.maximum(
                old, jnp.broadcast_to(jnp.max(scores, axis=1, keepdims=True), (rows, size))
            )
            probs[j] = jnp.exp2((scores - wide(highest, rows)) * factor).astype(jnp.bfloat16)
            top[h] = jnp.exp2((old - highest) * factor)
        landed(da, at, 2 * g + 1).wait_recv()
        values = kv[da, at, 2 * g + 1, :rows, :]
        values = jnp.concatenate([values, jnp.ones_like(values)], axis=1)
        for j in range(group):
            h = g * group + j
            product = jnp.dot(probs[j], values, preferred_element_type=jnp.float32)
            close(h, acc[h] * wide(top[h], 2 * size) + product)
        keep(g)

    def pass_on(da, *which):
        @pl.when(a >= da)
        def _():
            for p in which:
                landed(da, b, p).wait_recv()
                spread(da, p, lambda copy: copy.start())

    def column_block(da, g):
        @pl.when(a >= da)
        def _():
            attend(da, b, g)

    def inner_blocks(da, g, last=False):
        if last:
            steps = inner - 1
        else:
            steps = inner
        if inner == 1:
            return

        def one(step, carry):
            at = (b + step) % inner

            @pl.when((a >= da) & needed(da, at, b))
            def _():
                for p in (2 * g, 2 * g + 1):
                    landed(da, at, p).wait_recv()
                attend(da, at, g)

            return carry

        if steps > 1:
            lax.fori_loop(1, steps, one, 0)
        if last:
            @pl.when(a >= da)
            def _():
                attend_last(da, (b + inner - 1) % inner, g)

            @pl.when(a < da)
            def _():
                finish(g)

    def give(h, to):
        return pltpu.make_async_remote_copy(
            src_ref=done.at[h, pl.ds(to * out_rows, out_rows)],
            dst_ref=out_ref.at[:, pl.ds(pl.multiple_of((place * q_heads + h) * size, size), size)],
            send_sem=out_send.at[h, to],
            recv_sem=out_recv.at[h, place],
            device_id={"head": to},
            device_id_type=MESH,
        )

    def taken(h, source):
        return pltpu.make_async_remote_copy(
            src_ref=done.at[h, pl.ds(0, out_rows)],
            dst_ref=out_ref.at[:, pl.ds(pl.multiple_of((source * q_heads + h) * size, size), size)],
            send_sem=out_send.at[h, source],
            recv_sem=out_recv.at[h, source],
            device_id={"head": source},
            device_id_type=MESH,
        )

    def close(h, total):
        done[h] = (total[:, :size] / total[:, size:]).astype(jnp.bfloat16)
        for step in range(1, heads):
            give(h, (place + step) % heads).start()

    def keep(g):
        for j in range(group):
            h = g * group + j
            out_ref[:, pl.ds(pl.multiple_of((place * q_heads + h) * size, size), size)] = done[
                h, pl.ds(pl.multiple_of(place * out_rows, out_rows), out_rows), :
            ]

    def finish(g):
        for j in range(group):
            close(g * group + j, acc[g * group + j])
        keep(g)

    groups = range(kv_heads)
    for g in groups:
        attend(0, b, g, first=True)
    for da in range(1, reach):
        pass_on(da, 0, 1)
        for g in groups:
            column_block(da, g)
            if g + 1 < kv_heads:
                inner_blocks(da - 1, g)
                pass_on(da, 2 * g + 2, 2 * g + 3)
            else:
                inner_blocks(da - 1, g)

    @pl.when(b > 0)
    def _():
        pass_on(reach, 0, 1)
        for g in groups:
            column_block(reach, g)
            if g + 1 < kv_heads:
                pass_on(reach, 2 * g + 2, 2 * g + 3)
            inner_blocks(reach, g)
            if reach > 1 and inner > 1:
                inner_blocks(reach - 1, g, last=True)
            else:
                inner_blocks(reach - 1, g)
                finish(g)

    @pl.when(b == 0)
    def _():
        for g in groups:
            inner_blocks(reach - 1, g)
        for g in groups:
            pass_on(reach, 2 * g, 2 * g + 1)
            column_block(reach, g)
            if inner > 1:
                inner_blocks(reach, g, last=True)
            else:
                finish(g)

    for h in range(q_heads):
        for step in range(1, heads):
            taken(h, (place + step) % heads).wait_recv()
    for da in range(reach + 1):
        @pl.when(a >= da)
        def _():
            for p in range(pieces):
                spread(da, p, lambda copy: copy.wait_send())
    for h in range(q_heads):
        for step in range(1, heads):
            give(h, (place + step) % heads).wait_send()


def in_hbm(array):
    return pltpu.with_memory_space_constraint(array, pltpu.HBM)


def local(outer, inner, heads, queries, keys, values, doc_ids):
    rows, q_heads, size = queries.shape
    kv_heads = keys.shape[1]
    reach = outer // 2
    return pl.pallas_call(
        functools.partial(kernel, outer, inner, heads),
        out_shape=jax.ShapeDtypeStruct((rows // heads, heads * q_heads * size), jnp.bfloat16),
        in_specs=[pl.BlockSpec(memory_space=pltpu.HBM)] * 4,
        out_specs=pl.BlockSpec(memory_space=pltpu.VMEM),
        scratch_shapes=[
            pltpu.VMEM((rows * q_heads, size), jnp.bfloat16),
            pltpu.VMEM((rows * kv_heads, size), jnp.bfloat16),
            pltpu.VMEM((rows * kv_heads, size), jnp.bfloat16),
            pltpu.VMEM((rows // size, size), jnp.int32),
            pltpu.SemaphoreType.DMA((4,)),
            pltpu.VMEM((reach + 1, inner, 2 * kv_heads, rows + ID_ROWS, size), jnp.bfloat16),
            pltpu.VMEM((q_heads, rows, size), jnp.bfloat16),
            pltpu.VMEM((q_heads, rows, size), jnp.float32),
            pltpu.VMEM((q_heads, rows, 2 * size), jnp.float32),
            pltpu.VMEM((q_heads // kv_heads, rows, rows), jnp.bfloat16),
            pltpu.VMEM((q_heads, rows, size), jnp.bfloat16),
            pltpu.VMEM((rows, size), jnp.float32),
            pltpu.SemaphoreType.DMA((reach, 2 * kv_heads)),
            pltpu.SemaphoreType.DMA((reach + 1, inner, 2 * kv_heads)),
            pltpu.SemaphoreType.DMA((inner,)),
            pltpu.SemaphoreType.DMA((reach + 1, inner, 2 * kv_heads)),
            pltpu.SemaphoreType.DMA((q_heads, heads)),
            pltpu.SemaphoreType.DMA((q_heads, heads)),
        ],
        compiler_params=pltpu.CompilerParams(
            collective_id=0, has_side_effects=True, vmem_limit_bytes=48 * 1024 * 1024
        ),
    )(
        in_hbm(queries.reshape(rows * q_heads, size)),
        in_hbm(keys.reshape(rows * kv_heads, size)),
        in_hbm(values.reshape(rows * kv_heads, size)),
        in_hbm(doc_ids.reshape(rows // size, size)),
    )


def solution(mesh):
    inner = inner_size(mesh)
    return jax.shard_map(
        functools.partial(local, mesh.shape["ctx"] // inner, inner, mesh.shape["head"]),
        mesh=mesh,
        in_specs=(P("ctx", "head", None), P("ctx", "head", None), P("ctx", "head", None), P("ctx")),
        out_specs=P(("ctx", "head"), None),
        check_vma=False,
    )
```

```python
import functools
import math

import jax
import jax.numpy as jnp
from jax import lax
from jax.experimental import pallas as pl
from jax.experimental.pallas import tpu as pltpu
from jax.sharding import PartitionSpec as P

MESH = pl.DeviceIdType.MESH
HIDDEN = -1e30
ONE_ROWS = 16
ID_ROWS = 16


def inner_size(mesh):
    axes = list(mesh.axis_names)
    column = mesh.devices if axes.index("ctx") == 0 else mesh.devices.T
    places = [getattr(device, "coords", None) for device in column[:, 0]]
    count = len(places)
    if count < 2 or any(place is None for place in places):
        return 1
    moved = [i for i in range(len(places[0])) if places[0][i] != places[1][i]]
    if len(moved) != 1:
        return 1
    inner = len({place[moved[0]] for place in places})
    return inner if count % (2 * inner) == 0 else 1


def kernel(
    outer, inner, heads,
    q_hbm, k_hbm, v_hbm, id_hbm, out_ref,
    q_ref, k_ref, v_ref, id_ref, loaded, ks, vs, qs, top, acc, done,
    along_send, across_send, block_recv, out_send, out_recv,
):
    reach = outer // 2
    q_heads, rows, size = qs.shape
    kv_heads = ks.shape[2]
    group = q_heads // kv_heads
    out_rows = out_ref.shape[0]
    pieces = 2 * kv_heads
    factor = size ** -0.5 * math.log2(math.e)

    me = lax.axis_index("ctx")
    a, b = me // inner, me % inner
    place = lax.axis_index("head")
    has_prev, has_next = a > 0, a < outer - 1

    def block(da, at, p):
        if p % 2:
            return vs.at[da, at, p // 2]
        return ks.at[da, at, p // 2, pl.ds(0, rows + ID_ROWS if p == 0 else rows)]

    loads = [
        pltpu.make_async_copy(source, held, loaded.at[i])
        for i, (source, held) in enumerate(
            ((k_hbm, k_ref), (v_hbm, v_ref), (id_hbm, id_ref), (q_hbm, q_ref))
        )
    ]
    for load in loads:
        load.start()

    barrier = pltpu.get_barrier_semaphore()

    def greet(device_id):
        pl.semaphore_signal(barrier, inc=1, device_id=device_id, device_id_type=MESH)

    @pl.when(has_prev)
    def _():
        greet({"ctx": me - inner})

    @pl.when(has_next)
    def _():
        greet({"ctx": me + inner})

    for step in range(1, inner):
        greet({"ctx": a * inner + (b + step) % inner})
    for step in range(1, heads):
        greet({"head": (place + step) % heads})

    def split_heads(ref, count, store):
        chunk = min(256, ref.shape[0])
        tokens = chunk // count
        row = lax.broadcasted_iota(jnp.int32, (chunk, chunk), 0)
        col = lax.broadcasted_iota(jnp.int32, (chunk, chunk), 1)
        order = jnp.where(col == (row % tokens) * count + row // tokens, 1.0, 0.0).astype(jnp.bfloat16)
        for i in range(ref.shape[0] // chunk):
            part = ref[i * chunk:(i + 1) * chunk, :]
            moved = jnp.dot(order, part, preferred_element_type=jnp.float32)
            for h in range(count):
                store(h, pl.ds(i * tokens, tokens), moved[h * tokens:(h + 1) * tokens])

    def store_k(h, where, value):
        ks[0, b, h, where, :] = value.astype(jnp.bfloat16)

    def store_v(h, where, value):
        vs[0, b, h, :, where] = value.T.astype(jnp.bfloat16)

    def store_q(h, where, value):
        qs[h, where, :] = value.astype(jnp.bfloat16)

    loads[0].wait()
    split_heads(k_ref, kv_heads, store_k)
    loads[1].wait()
    split_heads(v_ref, kv_heads, store_v)
    loads[2].wait()
    numbers = id_ref[...].astype(jnp.float32)
    line = lax.broadcasted_iota(jnp.int32, (ID_ROWS, size), 0)
    lines = jnp.zeros((ID_ROWS, size), jnp.float32)
    for i in range(rows // size):
        lines = jnp.where(line == i, numbers[i:i + 1, :], lines)
    ks[0, b, 0, rows:rows + ID_ROWS, :] = lines.astype(jnp.bfloat16)

    greeted = has_prev.astype(jnp.int32) + has_next.astype(jnp.int32) + (inner - 1) + (heads - 1)
    pl.semaphore_wait(barrier, greeted)

    def along(da, p):
        return pltpu.make_async_remote_copy(
            src_ref=block(da, b, p),
            dst_ref=block(da + 1, b, p),
            send_sem=along_send.at[da, p],
            recv_sem=block_recv.at[da + 1, b, p],
            device_id={"ctx": me + inner},
            device_id_type=MESH,
        )

    def across(da, p, to):
        return pltpu.make_async_remote_copy(
            src_ref=block(da, b, p),
            dst_ref=block(da, b, p),
            send_sem=across_send.at[da, to, p],
            recv_sem=block_recv.at[da, b, p],
            device_id={"ctx": a * inner + to},
            device_id_type=MESH,
        )

    def landed(da, at, p):
        return pltpu.make_async_remote_copy(
            src_ref=block(da, at, p),
            dst_ref=block(da, at, p),
            send_sem=along_send.at[0, p],
            recv_sem=block_recv.at[da, at, p],
            device_id={"ctx": me},
            device_id_type=MESH,
        )

    def needed(da, src, dst):
        if da == 0:
            return src < dst
        if da == reach:
            return src > dst
        return src != dst

    def spread(da, p, act):
        if da < reach:
            @pl.when(has_next)
            def _():
                act(along(da, p))
        for step in range(1, inner):
            to = (b + step) % inner

            @pl.when(needed(da, b, to))
            def _():
                act(across(da, p, to))

    for p in range(pieces):
        spread(0, p, lambda copy: copy.start())

    loads[3].wait()
    split_heads(q_ref, q_heads, store_q)

    row = lax.broadcasted_iota(jnp.int32, (rows, rows), 0)
    col = lax.broadcasted_iota(jnp.int32, (rows, rows), 1)

    def ids_line(da, at):
        held = ks[da, at, 0, rows:rows + ID_ROWS, :].astype(jnp.float32)
        return jnp.concatenate([held[i:i + 1, :] for i in range(rows // size)], axis=1)

    def attend(da, at, g, first=False):
        key_ids = jnp.sum(jnp.where(row == col, ids_line(da, at), 0.0), axis=1, keepdims=True)
        same = key_ids == ids_line(0, b)
        if first:
            same = same & (row <= col)
        bias = jnp.where(same, 0.0, HIDDEN)
        keys = ks[da, at, g, :rows, :]
        values = jnp.concatenate([vs[da, at, g], jnp.ones((ONE_ROWS, rows), jnp.bfloat16)], axis=0)
        for j in range(group):
            h = g * group + j
            scores = lax.dot_general(
                keys, qs[h], (((1,), (1,)), ((), ())), preferred_element_type=jnp.float32
            ) + bias
            highest = jnp.max(scores, axis=0, keepdims=True)
            if not first:
                old = top[h]
                highest = jnp.maximum(old, highest)
            weights = jnp.exp2((scores - highest) * factor).astype(jnp.bfloat16)
            product = jnp.dot(values, weights, preferred_element_type=jnp.float32)
            if not first:
                product = acc[h] * jnp.exp2((old - highest) * factor) + product
            top[h] = highest
            acc[h] = product

    def pass_on(da, *which):
        @pl.when(a >= da)
        def _():
            for p in which:
                landed(da, b, p).wait_recv()
                spread(da, p, lambda copy: copy.start())

    def column_block(da, g):
        @pl.when(a >= da)
        def _():
            attend(da, b, g)

    def inner_blocks(da, g):
        if inner == 1:
            return

        def one(step, carry):
            at = (b + step) % inner

            @pl.when((a >= da) & needed(da, at, b))
            def _():
                for p in (2 * g, 2 * g + 1):
                    landed(da, at, p).wait_recv()
                attend(da, at, g)

            return carry

        lax.fori_loop(1, inner, one, 0)

    def give(h, to):
        return pltpu.make_async_remote_copy(
            src_ref=done.at[h, pl.ds(to * out_rows, out_rows)],
            dst_ref=out_ref.at[:, pl.ds(pl.multiple_of((place * q_heads + h) * size, size), size)],
            send_sem=out_send.at[h, to],
            recv_sem=out_recv.at[h, place],
            device_id={"head": to},
            device_id_type=MESH,
        )

    def taken(h, source):
        return pltpu.make_async_remote_copy(
            src_ref=done.at[h, pl.ds(0, out_rows)],
            dst_ref=out_ref.at[:, pl.ds(pl.multiple_of((source * q_heads + h) * size, size), size)],
            send_sem=out_send.at[h, source],
            recv_sem=out_recv.at[h, source],
            device_id={"head": source},
            device_id_type=MESH,
        )

    def finish(g):
        for j in range(group):
            h = g * group + j
            total = acc[h]
            done[h] = (total[:size] / total[size:size + 1]).T.astype(jnp.bfloat16)
            for step in range(1, heads):
                give(h, (place + step) % heads).start()
        for j in range(group):
            h = g * group + j
            out_ref[:, pl.ds(pl.multiple_of((place * q_heads + h) * size, size), size)] = done[
                h, pl.ds(pl.multiple_of(place * out_rows, out_rows), out_rows), :
            ]

    groups = range(kv_heads)
    for g in groups:
        attend(0, b, g, first=True)
    for da in range(1, reach):
        pass_on(da, 0, 1)
        for g in groups:
            column_block(da, g)
            if g + 1 < kv_heads:
                inner_blocks(da - 1, g)
                pass_on(da, 2 * g + 2, 2 * g + 3)
            else:
                inner_blocks(da - 1, g)

    @pl.when(b > 0)
    def _():
        pass_on(reach, 0, 1)
        for g in groups:
            column_block(reach, g)
            if g + 1 < kv_heads:
                pass_on(reach, 2 * g + 2)
            inner_blocks(reach - 1, g)
            if g + 1 < kv_heads:
                pass_on(reach, 2 * g + 3)
            inner_blocks(reach, g)
            finish(g)

    @pl.when(b == 0)
    def _():
        for g in groups:
            inner_blocks(reach - 1, g)
        for g in groups:
            pass_on(reach, 2 * g, 2 * g + 1)
            column_block(reach, g)
            inner_blocks(reach, g)
            finish(g)

    for h in range(q_heads):
        for step in range(1, heads):
            taken(h, (place + step) % heads).wait_recv()
    for da in range(reach + 1):
        @pl.when(a >= da)
        def _():
            for p in range(pieces):
                spread(da, p, lambda copy: copy.wait_send())
    for h in range(q_heads):
        for step in range(1, heads):
            give(h, (place + step) % heads).wait_send()


def in_hbm(array):
    return pltpu.with_memory_space_constraint(array, pltpu.HBM)


def local(outer, inner, heads, queries, keys, values, doc_ids):
    rows, q_heads, size = queries.shape
    kv_heads = keys.shape[1]
    reach = outer // 2
    return pl.pallas_call(
        functools.partial(kernel, outer, inner, heads),
        out_shape=jax.ShapeDtypeStruct((rows // heads, heads * q_heads * size), jnp.bfloat16),
        in_specs=[pl.BlockSpec(memory_space=pltpu.HBM)] * 4,
        out_specs=pl.BlockSpec(memory_space=pltpu.VMEM),
        scratch_shapes=[
            pltpu.VMEM((rows * q_heads, size), jnp.bfloat16),
            pltpu.VMEM((rows * kv_heads, size), jnp.bfloat16),
            pltpu.VMEM((rows * kv_heads, size), jnp.bfloat16),
            pltpu.VMEM((rows // size, size), jnp.int32),
            pltpu.SemaphoreType.DMA((4,)),
            pltpu.VMEM((reach + 1, inner, kv_heads, rows + ID_ROWS, size), jnp.bfloat16),
            pltpu.VMEM((reach + 1, inner, kv_heads, size, rows), jnp.bfloat16),
            pltpu.VMEM((q_heads, rows, size), jnp.bfloat16),
            pltpu.VMEM((q_heads, 1, rows), jnp.float32),
            pltpu.VMEM((q_heads, size + ONE_ROWS, rows), jnp.float32),
            pltpu.VMEM((q_heads, rows, size), jnp.bfloat16),
            pltpu.SemaphoreType.DMA((reach, 2 * kv_heads)),
            pltpu.SemaphoreType.DMA((reach + 1, inner, 2 * kv_heads)),
            pltpu.SemaphoreType.DMA((reach + 1, inner, 2 * kv_heads)),
            pltpu.SemaphoreType.DMA((q_heads, heads)),
            pltpu.SemaphoreType.DMA((q_heads, heads)),
        ],
        compiler_params=pltpu.CompilerParams(
            collective_id=0, has_side_effects=True, vmem_limit_bytes=48 * 1024 * 1024
        ),
    )(
        in_hbm(queries.reshape(rows * q_heads, size)),
        in_hbm(keys.reshape(rows * kv_heads, size)),
        in_hbm(values.reshape(rows * kv_heads, size)),
        in_hbm(doc_ids.reshape(rows // size, size)),
    )


def solution(mesh):
    inner = inner_size(mesh)
    return jax.shard_map(
        functools.partial(local, mesh.shape["ctx"] // inner, inner, mesh.shape["head"]),
        mesh=mesh,
        in_specs=(P("ctx", "head", None), P("ctx", "head", None), P("ctx", "head", None), P("ctx")),
        out_specs=P(("ctx", "head"), None),
        check_vma=False,
    )
```

```python
import functools
import math

import jax
import jax.numpy as jnp
from jax import lax
from jax.experimental import pallas as pl
from jax.experimental.pallas import tpu as pltpu
from jax.sharding import PartitionSpec as P

MESH = pl.DeviceIdType.MESH
HIDDEN = -1e30
ID_ROWS = 16


def inner_size(mesh):
    axes = list(mesh.axis_names)
    column = mesh.devices if axes.index("ctx") == 0 else mesh.devices.T
    places = [getattr(device, "coords", None) for device in column[:, 0]]
    count = len(places)
    if count < 2 or any(place is None for place in places):
        return 1
    moved = [i for i in range(len(places[0])) if places[0][i] != places[1][i]]
    if len(moved) != 1:
        return 1
    inner = len({place[moved[0]] for place in places})
    return inner if count % (2 * inner) == 0 else 1


def kernel(
    outer, inner, heads,
    q_hbm, k_hbm, v_hbm, id_hbm, out_ref,
    q_ref, k_ref, v_ref, id_ref, loaded, kv, qs, top, acc, done, id_col,
    along_send, across_send, block_recv, out_send, out_recv,
):
    reach = outer // 2
    q_heads, rows, size = qs.shape
    kv_heads = kv.shape[2] // 2
    group = q_heads // kv_heads
    out_rows = out_ref.shape[0]
    factor = size ** -0.5 * math.log2(math.e)

    me = lax.axis_index("ctx")
    a, b = me // inner, me % inner
    place = lax.axis_index("head")
    has_prev, has_next = a > 0, a < outer - 1

    def span(kind):
        return pl.ds(0, rows + ID_ROWS) if kind == 0 else pl.ds(0, rows)

    loads = [
        pltpu.make_async_copy(source, held, loaded.at[i])
        for i, (source, held) in enumerate(
            ((k_hbm, k_ref), (v_hbm, v_ref), (id_hbm, id_ref), (q_hbm, q_ref))
        )
    ]
    for load in loads:
        load.start()

    barrier = pltpu.get_barrier_semaphore()

    def greet(device_id):
        pl.semaphore_signal(barrier, inc=1, device_id=device_id, device_id_type=MESH)

    @pl.when(has_prev)
    def _():
        greet({"ctx": me - inner})

    @pl.when(has_next)
    def _():
        greet({"ctx": me + inner})

    for step in range(1, inner):
        greet({"ctx": a * inner + (b + step) % inner})
    for step in range(1, heads):
        greet({"head": (place + step) % heads})

    def split_heads(ref, count, store):
        chunk = min(256, ref.shape[0])
        tokens = chunk // count
        row = lax.broadcasted_iota(jnp.int32, (chunk, chunk), 0)
        col = lax.broadcasted_iota(jnp.int32, (chunk, chunk), 1)
        order = jnp.where(col == (row % tokens) * count + row // tokens, 1.0, 0.0).astype(jnp.bfloat16)
        for i in range(ref.shape[0] // chunk):
            part = ref[i * chunk:(i + 1) * chunk, :]
            moved = jnp.dot(order, part, preferred_element_type=jnp.float32).astype(jnp.bfloat16)
            for h in range(count):
                store(h, pl.ds(i * tokens, tokens), moved[h * tokens:(h + 1) * tokens])

    def store_k(h, where, value):
        kv[0, b, 2 * h, where, :] = value

    def store_v(h, where, value):
        kv[0, b, 2 * h + 1, where, :] = value

    def store_q(h, where, value):
        qs[h, where, :] = value

    loads[0].wait()
    split_heads(k_ref, kv_heads, store_k)
    loads[1].wait()
    split_heads(v_ref, kv_heads, store_v)
    loads[2].wait()
    numbers = id_ref[...].astype(jnp.float32)
    line = lax.broadcasted_iota(jnp.int32, (ID_ROWS, size), 0)
    lines = jnp.zeros((ID_ROWS, size), jnp.float32)
    for i in range(rows // size):
        lines = jnp.where(line == i, numbers[i:i + 1, :], lines)
    for g in range(kv_heads):
        kv[0, b, 2 * g, rows:rows + ID_ROWS, :] = lines.astype(jnp.bfloat16)
    top[...] = jnp.full(top.shape, HIDDEN, jnp.float32)
    acc[...] = jnp.zeros(acc.shape, jnp.float32)

    greeted = has_prev.astype(jnp.int32) + has_next.astype(jnp.int32) + (inner - 1) + (heads - 1)
    pl.semaphore_wait(barrier, greeted)

    def along(da, g, kind):
        p = 2 * g + kind
        return pltpu.make_async_remote_copy(
            src_ref=kv.at[da, b, p, span(kind)],
            dst_ref=kv.at[da + 1, b, p, span(kind)],
            send_sem=along_send.at[da, p],
            recv_sem=block_recv.at[da + 1, b, p],
            device_id={"ctx": me + inner},
            device_id_type=MESH,
        )

    def across(da, g, kind, to):
        p = 2 * g + kind
        return pltpu.make_async_remote_copy(
            src_ref=kv.at[da, b, p, span(kind)],
            dst_ref=kv.at[da, b, p, span(kind)],
            send_sem=across_send.at[da, to, p],
            recv_sem=block_recv.at[da, b, p],
            device_id={"ctx": a * inner + to},
            device_id_type=MESH,
        )

    def landed(da, at, g, kind):
        p = 2 * g + kind
        return pltpu.make_async_remote_copy(
            src_ref=kv.at[da, at, p, span(kind)],
            dst_ref=kv.at[da, at, p, span(kind)],
            send_sem=along_send.at[0, p],
            recv_sem=block_recv.at[da, at, p],
            device_id={"ctx": me},
            device_id_type=MESH,
        )

    def needed(da, src, dst):
        return (src != dst) & ((da > 0) | (src < dst)) & ((da < reach) | (src > dst))

    def spread(da, g, kind, act):
        @pl.when(has_next & (da < reach))
        def _():
            act(along(da, g, kind))

        for step in range(1, inner):
            to = (b + step) % inner

            @pl.when(needed(da, b, to))
            def _():
                act(across(da, g, kind, to))

    for g in range(kv_heads):
        for kind in range(2):
            spread(0, g, kind, lambda copy: copy.start())

    loads[3].wait()
    split_heads(q_ref, q_heads, store_q)

    row = lax.broadcasted_iota(jnp.int32, (rows, rows), 0)
    col = lax.broadcasted_iota(jnp.int32, (rows, rows), 1)

    def key_ids(da, at):
        held = kv[da, at, 0, rows:rows + ID_ROWS, :].astype(jnp.float32)
        return jnp.concatenate([held[i:i + 1, :] for i in range(rows // size)], axis=1)

    own_ids = key_ids(0, b)
    column = jnp.sum(jnp.where(row == col, own_ids, 0.0), axis=1, keepdims=True)
    id_col[...] = jnp.broadcast_to(column, id_col.shape)

    def wide(value, width):
        return jnp.concatenate([value] * (width // value.shape[1]), axis=1)

    def attend(da, at, g):
        back = (me - (a - da) * inner - at) * rows
        visible = (wide(id_col[...], rows) == key_ids(da, at)) & (col - row <= back)
        bias = jnp.where(visible, 0.0, HIDDEN)
        keys = kv[da, at, 2 * g, :rows, :]
        values = kv[da, at, 2 * g + 1, :rows, :]
        values = jnp.concatenate([values, jnp.ones_like(values)], axis=1)
        for j in range(group):
            h = g * group + j
            scores = lax.dot_general(
                qs[h], keys, (((1,), (1,)), ((), ())), preferred_element_type=jnp.float32
            ) + bias
            old = top[h]
            highest = jnp.maximum(
                old, jnp.broadcast_to(jnp.max(scores, axis=1, keepdims=True), (rows, size))
            )
            weights = jnp.exp2((scores - wide(highest, rows)) * factor).astype(jnp.bfloat16)
            product = jnp.dot(weights, values, preferred_element_type=jnp.float32)
            acc[h] = acc[h] * wide(jnp.exp2((old - highest) * factor), 2 * size) + product
            top[h] = highest

    def give(h, to):
        return pltpu.make_async_remote_copy(
            src_ref=done.at[h, pl.ds(to * out_rows, out_rows)],
            dst_ref=out_ref.at[:, pl.ds(pl.multiple_of((place * q_heads + h) * size, size), size)],
            send_sem=out_send.at[h, to],
            recv_sem=out_recv.at[h, place],
            device_id={"head": to},
            device_id_type=MESH,
        )

    def taken(h, source):
        return pltpu.make_async_remote_copy(
            src_ref=done.at[h, pl.ds(0, out_rows)],
            dst_ref=out_ref.at[:, pl.ds(pl.multiple_of((source * q_heads + h) * size, size), size)],
            send_sem=out_send.at[h, source],
            recv_sem=out_recv.at[h, source],
            device_id={"head": source},
            device_id_type=MESH,
        )

    def finish(g):
        def one(j, carry):
            h = g * group + j
            total = acc[h]
            done[h] = (total[:, :size] / total[:, size:]).astype(jnp.bfloat16)
            for step in range(1, heads):
                give(h, (place + step) % heads).start()
            out_ref[:, pl.ds(pl.multiple_of((place * q_heads + h) * size, size), size)] = done[
                h, pl.ds(pl.multiple_of(place * out_rows, out_rows), out_rows), :
            ]
            return carry

        lax.fori_loop(0, group, one, 0)

    def order(first):
        steps = [dict(g=g) for g in range(kv_heads)]
        for da in range(1, reach):
            for g in range(kv_heads):
                steps.append(dict(take=3, take_da=da, take_g=g, da=da, g=g))
                steps.append(dict(others=1, da=da - 1, g=g))
        if first:
            for g in range(kv_heads):
                steps.append(dict(others=1, da=reach - 1, g=g))
            for g in range(kv_heads):
                steps.append(dict(take=3, take_da=reach, take_g=g, da=reach, g=g))
                steps.append(dict(others=1, da=reach, g=g, last=1))
        else:
            steps.append(dict(take=3, take_da=reach, take_g=0, da=reach, g=0))
            for g in range(kv_heads):
                more = int(g + 1 < kv_heads)
                steps.append(dict(take=more, take_da=reach, take_g=g + more, others=1, da=reach - 1, g=g))
                steps.append(dict(take=2 * more, take_da=reach, take_g=g + more, others=1, da=reach, g=g, last=1))
                if more:
                    steps.append(dict(da=reach, g=g + 1))
        return steps

    orders = order(True), order(False)
    step_count = len(orders[0])
    fields = ("take", "take_da", "take_g", "others", "da", "g", "last")
    base = 1 + max(3, reach, kv_heads)

    def coded(step):
        code = 0
        for name in fields:
            code = code * base + step.get(name, 0)
        return code

    def body(i, carry):
        code = jnp.int32(0)
        for n in range(step_count):
            both = [coded(steps[n]) for steps in orders]
            code = jnp.where(i == n, jnp.where(b == 0, both[0], both[1]), code)
        now = {}
        for name in reversed(fields):
            now[name] = code % base
            code = code // base
        take, take_da, take_g = now["take"], now["take_da"], now["take_g"]
        others, da, g = now["others"], now["da"], now["g"]

        for kind in range(2):
            @pl.when((take // (1 + kind) % 2 == 1) & (a >= take_da))
            def _():
                landed(take_da, b, take_g, kind).wait_recv()
                spread(take_da, take_g, kind, lambda copy: copy.start())

        def one(step, carry):
            at = (b + step) % inner

            @pl.when((a >= da) & ((step == 0) | needed(da, at, b)))
            def _():
                @pl.when(step > 0)
                def _():
                    for kind in range(2):
                        landed(da, at, g, kind).wait_recv()

                attend(da, at, g)

            return carry

        lax.fori_loop(others, jnp.where(others == 1, inner, 1), one, 0)

        @pl.when(now["last"] == 1)
        def _():
            finish(g)

        return carry

    lax.fori_loop(0, step_count, body, 0)

    for h in range(q_heads):
        for step in range(1, heads):
            taken(h, (place + step) % heads).wait_recv()
    for da in range(reach + 1):
        @pl.when(a >= da)
        def _():
            for g in range(kv_heads):
                for kind in range(2):
                    spread(da, g, kind, lambda copy: copy.wait_send())
    for h in range(q_heads):
        for step in range(1, heads):
            give(h, (place + step) % heads).wait_send()


def in_hbm(array):
    return pltpu.with_memory_space_constraint(array, pltpu.HBM)


def local(outer, inner, heads, queries, keys, values, doc_ids):
    rows, q_heads, size = queries.shape
    kv_heads = keys.shape[1]
    reach = outer // 2
    return pl.pallas_call(
        functools.partial(kernel, outer, inner, heads),
        out_shape=jax.ShapeDtypeStruct((rows // heads, heads * q_heads * size), jnp.bfloat16),
        in_specs=[pl.BlockSpec(memory_space=pltpu.HBM)] * 4,
        out_specs=pl.BlockSpec(memory_space=pltpu.VMEM),
        scratch_shapes=[
            pltpu.VMEM((rows * q_heads, size), jnp.bfloat16),
            pltpu.VMEM((rows * kv_heads, size), jnp.bfloat16),
            pltpu.VMEM((rows * kv_heads, size), jnp.bfloat16),
            pltpu.VMEM((rows // size, size), jnp.int32),
            pltpu.SemaphoreType.DMA((4,)),
            pltpu.VMEM((reach + 1, inner, 2 * kv_heads, rows + ID_ROWS, size), jnp.bfloat16),
            pltpu.VMEM((q_heads, rows, size), jnp.bfloat16),
            pltpu.VMEM((q_heads, rows, size), jnp.float32),
            pltpu.VMEM((q_heads, rows, 2 * size), jnp.float32),
            pltpu.VMEM((q_heads, rows, size), jnp.bfloat16),
            pltpu.VMEM((rows, size), jnp.float32),
            pltpu.SemaphoreType.DMA((reach + 1, 2 * kv_heads)),
            pltpu.SemaphoreType.DMA((reach + 1, inner, 2 * kv_heads)),
            pltpu.SemaphoreType.DMA((reach + 1, inner, 2 * kv_heads)),
            pltpu.SemaphoreType.DMA((q_heads, heads)),
            pltpu.SemaphoreType.DMA((q_heads, heads)),
        ],
        compiler_params=pltpu.CompilerParams(
            collective_id=0, has_side_effects=True, vmem_limit_bytes=48 * 1024 * 1024
        ),
    )(
        in_hbm(queries.reshape(rows * q_heads, size)),
        in_hbm(keys.reshape(rows * kv_heads, size)),
        in_hbm(values.reshape(rows * kv_heads, size)),
        in_hbm(doc_ids.reshape(rows // size, size)),
    )


def solution(mesh):
    inner = inner_size(mesh)
    return jax.shard_map(
        functools.partial(local, mesh.shape["ctx"] // inner, inner, mesh.shape["head"]),
        mesh=mesh,
        in_specs=(P("ctx", "head", None), P("ctx", "head", None), P("ctx", "head", None), P("ctx")),
        out_specs=P(("ctx", "head"), None),
        check_vma=False,
    )
```

```python
import functools
import math

import jax
import jax.numpy as jnp
from jax import lax
from jax.experimental import pallas as pl
from jax.experimental.pallas import tpu as pltpu
from jax.sharding import PartitionSpec as P

MESH = pl.DeviceIdType.MESH
HIDDEN = -1e30
ID_ROWS = 16


def inner_size(mesh):
    axes = list(mesh.axis_names)
    column = mesh.devices if axes.index("ctx") == 0 else mesh.devices.T
    places = [getattr(device, "coords", None) for device in column[:, 0]]
    count = len(places)
    if count < 2 or any(place is None for place in places):
        return 1
    moved = [i for i in range(len(places[0])) if places[0][i] != places[1][i]]
    if len(moved) != 1:
        return 1
    inner = len({place[moved[0]] for place in places})
    return inner if count % (4 * inner) == 0 else 1


def kernel(
    outer, inner, heads,
    q_hbm, k_hbm, v_hbm, id_hbm, out_ref,
    q_ref, k_ref, v_ref, id_ref, loaded, kv, qs, top, acc, probs, done, id_col,
    along_send, across_send, block_recv, out_send, out_recv,
):
    reach = outer // 2
    q_heads, rows, size = qs.shape
    kv_heads = kv.shape[2] // 2
    group = q_heads // kv_heads
    out_rows = out_ref.shape[0]
    pieces = 2 * kv_heads
    factor = size ** -0.5 * math.log2(math.e)

    me = lax.axis_index("ctx")
    a, b = me // inner, me % inner
    place = lax.axis_index("head")
    has_prev, has_next = a > 0, a < outer - 1

    def span(p):
        return pl.ds(0, rows + ID_ROWS) if p == 0 else pl.ds(0, rows)

    loads = [
        pltpu.make_async_copy(source, held, loaded.at[i])
        for i, (source, held) in enumerate(
            ((k_hbm, k_ref), (v_hbm, v_ref), (id_hbm, id_ref), (q_hbm, q_ref))
        )
    ]
    for load in loads:
        load.start()

    barrier = pltpu.get_barrier_semaphore()

    def greet(device_id):
        pl.semaphore_signal(barrier, inc=1, device_id=device_id, device_id_type=MESH)

    @pl.when(has_prev)
    def _():
        greet({"ctx": me - inner})

    @pl.when(has_next)
    def _():
        greet({"ctx": me + inner})

    for step in range(1, inner):
        greet({"ctx": a * inner + (b + step) % inner})
    for step in range(1, heads):
        greet({"head": (place + step) % heads})

    def split_heads(ref, count, store):
        chunk = min(256, ref.shape[0])
        tokens = chunk // count
        row = lax.broadcasted_iota(jnp.int32, (chunk, chunk), 0)
        col = lax.broadcasted_iota(jnp.int32, (chunk, chunk), 1)
        order = jnp.where(col == (row % tokens) * count + row // tokens, 1.0, 0.0).astype(jnp.bfloat16)
        for i in range(ref.shape[0] // chunk):
            part = ref[i * chunk:(i + 1) * chunk, :]
            moved = jnp.dot(order, part, preferred_element_type=jnp.float32).astype(jnp.bfloat16)
            for h in range(count):
                store(h, pl.ds(i * tokens, tokens), moved[h * tokens:(h + 1) * tokens])

    def store_k(h, where, value):
        kv[0, b, 2 * h, where, :] = value

    def store_v(h, where, value):
        kv[0, b, 2 * h + 1, where, :] = value

    def store_q(h, where, value):
        qs[h, where, :] = value

    loads[0].wait()
    split_heads(k_ref, kv_heads, store_k)
    loads[1].wait()
    split_heads(v_ref, kv_heads, store_v)
    loads[2].wait()
    numbers = id_ref[...].astype(jnp.float32)
    line = lax.broadcasted_iota(jnp.int32, (ID_ROWS, size), 0)
    lines = jnp.zeros((ID_ROWS, size), jnp.float32)
    for i in range(rows // size):
        lines = jnp.where(line == i, numbers[i:i + 1, :], lines)
    kv[0, b, 0, rows:rows + ID_ROWS, :] = lines.astype(jnp.bfloat16)

    up, down = has_next.astype(jnp.int32), has_prev.astype(jnp.int32)
    greeted = up + down + (inner - 1) + (heads - 1)
    pl.semaphore_wait(barrier, greeted)

    def along(da, p):
        return pltpu.make_async_remote_copy(
            src_ref=kv.at[da, b, p, span(p)],
            dst_ref=kv.at[da + 1, b, p, span(p)],
            send_sem=along_send.at[da, p],
            recv_sem=block_recv.at[da + 1, b, p],
            device_id={"ctx": me + inner},
            device_id_type=MESH,
        )

    def across(da, p, to):
        return pltpu.make_async_remote_copy(
            src_ref=kv.at[da, b, p, span(p)],
            dst_ref=kv.at[da, b, p, span(p)],
            send_sem=across_send.at[da, to, p],
            recv_sem=block_recv.at[da, b, p],
            device_id={"ctx": a * inner + to},
            device_id_type=MESH,
        )

    def landed(da, at, p):
        return pltpu.make_async_remote_copy(
            src_ref=kv.at[da, at, p, span(p)],
            dst_ref=kv.at[da, at, p, span(p)],
            send_sem=along_send.at[0, p],
            recv_sem=block_recv.at[da, at, p],
            device_id={"ctx": me},
            device_id_type=MESH,
        )

    def needed(da, src, dst):
        if da == 0:
            return src < dst
        if da == reach:
            return src > dst
        return src != dst

    def spread(da, p, act):
        if da < reach:
            @pl.when(has_next)
            def _():
                act(along(da, p))
        for step in range(1, inner):
            to = (b + step) % inner

            @pl.when(needed(da, b, to))
            def _():
                act(across(da, p, to))

    for p in (0, 1):
        spread(0, p, lambda copy: copy.start())

    loads[3].wait()
    split_heads(q_ref, q_heads, store_q)

    row = lax.broadcasted_iota(jnp.int32, (rows, rows), 0)
    col = lax.broadcasted_iota(jnp.int32, (rows, rows), 1)

    def key_ids(da, at):
        held = kv[da, at, 0, rows:rows + ID_ROWS, :].astype(jnp.float32)
        return jnp.concatenate([held[i:i + 1, :] for i in range(rows // size)], axis=1)

    own_ids = key_ids(0, b)
    column = jnp.sum(jnp.where(row == col, own_ids, 0.0), axis=1, keepdims=True)
    id_col[...] = jnp.broadcast_to(column, id_col.shape)

    def wide(value, width):
        return jnp.concatenate([value] * (width // value.shape[1]), axis=1)

    def attend(da, at, g, first=False):
        same = wide(id_col[...], rows) == key_ids(da, at)
        if first:
            same = same & (col <= row)
        bias = jnp.where(same, 0.0, HIDDEN)
        keys = kv[da, at, 2 * g, :rows, :]
        values = kv[da, at, 2 * g + 1, :rows, :]
        values = jnp.concatenate([values, jnp.ones_like(values)], axis=1)
        for j in range(group):
            h = g * group + j
            scores = lax.dot_general(
                qs[h], keys, (((1,), (1,)), ((), ())), preferred_element_type=jnp.float32
            ) + bias
            highest = jnp.broadcast_to(jnp.max(scores, axis=1, keepdims=True), (rows, size))
            if not first:
                old = top[h]
                highest = jnp.maximum(old, highest)
            weights = jnp.exp2((scores - wide(highest, rows)) * factor).astype(jnp.bfloat16)
            product = jnp.dot(weights, values, preferred_element_type=jnp.float32)
            if not first:
                product = acc[h] * wide(jnp.exp2((old - highest) * factor), 2 * size) + product
            top[h] = highest
            acc[h] = product

    def attend_last(da, at, g):
        landed(da, at, 2 * g).wait_recv()
        bias = jnp.where(wide(id_col[...], rows) == key_ids(da, at), 0.0, HIDDEN)
        keys = kv[da, at, 2 * g, :rows, :]
        for j in range(group):
            h = g * group + j
            scores = lax.dot_general(
                qs[h], keys, (((1,), (1,)), ((), ())), preferred_element_type=jnp.float32
            ) + bias
            old = top[h]
            highest = jnp.maximum(
                old, jnp.broadcast_to(jnp.max(scores, axis=1, keepdims=True), (rows, size))
            )
            probs[j] = jnp.exp2((scores - wide(highest, rows)) * factor).astype(jnp.bfloat16)
            top[h] = jnp.exp2((old - highest) * factor)
        landed(da, at, 2 * g + 1).wait_recv()
        values = kv[da, at, 2 * g + 1, :rows, :]
        values = jnp.concatenate([values, jnp.ones_like(values)], axis=1)
        for j in range(group):
            h = g * group + j
            product = jnp.dot(probs[j], values, preferred_element_type=jnp.float32)
            close(h, acc[h] * wide(top[h], 2 * size) + product)
        keep(g)

    def pass_on(da, *which):
        @pl.when(a >= da)
        def _():
            for p in which:
                landed(da, b, p).wait_recv()
                spread(da, p, lambda copy: copy.start())

    def column_block(da, g):
        @pl.when(a >= da)
        def _():
            attend(da, b, g)

    def inner_blocks(da, g, last=False):
        if last:
            steps = inner - 1
        else:
            steps = inner
        if inner == 1:
            return

        def one(step, carry):
            at = (b + step) % inner

            @pl.when((a >= da) & needed(da, at, b))
            def _():
                for p in (2 * g, 2 * g + 1):
                    landed(da, at, p).wait_recv()
                attend(da, at, g)

            return carry

        if steps > 1:
            lax.fori_loop(1, steps, one, 0)
        if last:
            @pl.when(a >= da)
            def _():
                attend_last(da, (b + inner - 1) % inner, g)

            @pl.when(a < da)
            def _():
                finish(g)

    def give(h, to):
        return pltpu.make_async_remote_copy(
            src_ref=done.at[h, pl.ds(to * out_rows, out_rows)],
            dst_ref=out_ref.at[:, pl.ds(pl.multiple_of((place * q_heads + h) * size, size), size)],
            send_sem=out_send.at[h, to],
            recv_sem=out_recv.at[h, place],
            device_id={"head": to},
            device_id_type=MESH,
        )

    def taken(h, source):
        return pltpu.make_async_remote_copy(
            src_ref=done.at[h, pl.ds(0, out_rows)],
            dst_ref=out_ref.at[:, pl.ds(pl.multiple_of((source * q_heads + h) * size, size), size)],
            send_sem=out_send.at[h, source],
            recv_sem=out_recv.at[h, source],
            device_id={"head": source},
            device_id_type=MESH,
        )

    def close(h, total):
        done[h] = (total[:, :size] / total[:, size:]).astype(jnp.bfloat16)
        for step in range(1, heads):
            give(h, (place + step) % heads).start()

    def keep(g):
        for j in range(group):
            h = g * group + j
            out_ref[:, pl.ds(pl.multiple_of((place * q_heads + h) * size, size), size)] = done[
                h, pl.ds(pl.multiple_of(place * out_rows, out_rows), out_rows), :
            ]

    def finish(g):
        for j in range(group):
            close(g * group + j, acc[g * group + j])
        keep(g)

    groups = range(kv_heads)
    for g in groups:
        attend(0, b, g, first=True)
    def enter(g):
        pass_on(1, 2 * g, 2 * g + 1)
        if g + 1 < kv_heads:
            for p in (2 * g + 2, 2 * g + 3):
                spread(0, p, lambda copy: copy.start())
        column_block(1, g)

    enter(0)
    for g in groups:
        inner_blocks(0, g)
        for da in range(2, reach + 1):
            @pl.when(b > 0)
            def _():
                pass_on(da, 2 * g, 2 * g + 1)
                column_block(da, g)
                if da < reach:
                    inner_blocks(da - 1, g)

            @pl.when(b == 0)
            def _():
                inner_blocks(da - 1, g)
                pass_on(da, 2 * g, 2 * g + 1)
                column_block(da, g)

        if g + 1 < kv_heads:
            enter(g + 1)
        if inner > 1:
            @pl.when(b > 0)
            def _():
                inner_blocks(reach, g)
                inner_blocks(reach - 1, g, last=True)

            @pl.when(b == 0)
            def _():
                inner_blocks(reach, g, last=True)
        else:
            finish(g)

    for h in range(q_heads):
        for step in range(1, heads):
            taken(h, (place + step) % heads).wait_recv()
    for da in range(reach + 1):
        @pl.when(a >= da)
        def _():
            for p in range(pieces):
                spread(da, p, lambda copy: copy.wait_send())
    for h in range(q_heads):
        for step in range(1, heads):
            give(h, (place + step) % heads).wait_send()


def in_hbm(array):
    return pltpu.with_memory_space_constraint(array, pltpu.HBM)


def local(outer, inner, heads, queries, keys, values, doc_ids):
    rows, q_heads, size = queries.shape
    kv_heads = keys.shape[1]
    reach = outer // 2
    return pl.pallas_call(
        functools.partial(kernel, outer, inner, heads),
        out_shape=jax.ShapeDtypeStruct((rows // heads, heads * q_heads * size), jnp.bfloat16),
        in_specs=[pl.BlockSpec(memory_space=pltpu.HBM)] * 4,
        out_specs=pl.BlockSpec(memory_space=pltpu.VMEM),
        scratch_shapes=[
            pltpu.VMEM((rows * q_heads, size), jnp.bfloat16),
            pltpu.VMEM((rows * kv_heads, size), jnp.bfloat16),
            pltpu.VMEM((rows * kv_heads, size), jnp.bfloat16),
            pltpu.VMEM((rows // size, size), jnp.int32),
            pltpu.SemaphoreType.DMA((4,)),
            pltpu.VMEM((reach + 1, inner, 2 * kv_heads, rows + ID_ROWS, size), jnp.bfloat16),
            pltpu.VMEM((q_heads, rows, size), jnp.bfloat16),
            pltpu.VMEM((q_heads, rows, size), jnp.float32),
            pltpu.VMEM((q_heads, rows, 2 * size), jnp.float32),
            pltpu.VMEM((q_heads // kv_heads, rows, rows), jnp.bfloat16),
            pltpu.VMEM((q_heads, rows, size), jnp.bfloat16),
            pltpu.VMEM((rows, size), jnp.float32),
            pltpu.SemaphoreType.DMA((reach, 2 * kv_heads)),
            pltpu.SemaphoreType.DMA((reach + 1, inner, 2 * kv_heads)),
            pltpu.SemaphoreType.DMA((reach + 1, inner, 2 * kv_heads)),
            pltpu.SemaphoreType.DMA((q_heads, heads)),
            pltpu.SemaphoreType.DMA((q_heads, heads)),
        ],
        compiler_params=pltpu.CompilerParams(
            collective_id=0, has_side_effects=True, vmem_limit_bytes=48 * 1024 * 1024
        ),
    )(
        in_hbm(queries.reshape(rows * q_heads, size)),
        in_hbm(keys.reshape(rows * kv_heads, size)),
        in_hbm(values.reshape(rows * kv_heads, size)),
        in_hbm(doc_ids.reshape(rows // size, size)),
    )


def solution(mesh):
    inner = inner_size(mesh)
    return jax.shard_map(
        functools.partial(local, mesh.shape["ctx"] // inner, inner, mesh.shape["head"]),
        mesh=mesh,
        in_specs=(P("ctx", "head", None), P("ctx", "head", None), P("ctx", "head", None), P("ctx")),
        out_specs=P(("ctx", "head"), None),
        check_vma=False,
    )
```

```python
import functools
import math

import jax
import jax.numpy as jnp
from jax import lax
from jax.experimental import pallas as pl
from jax.experimental.pallas import tpu as pltpu
from jax.sharding import PartitionSpec as P

MESH = pl.DeviceIdType.MESH
HIDDEN = -1e30
ID_ROWS = 16


def inner_size(mesh):
    axes = list(mesh.axis_names)
    column = mesh.devices if axes.index("ctx") == 0 else mesh.devices.T
    places = [getattr(device, "coords", None) for device in column[:, 0]]
    count = len(places)
    if count < 2 or any(place is None for place in places):
        return 1
    moved = [i for i in range(len(places[0])) if places[0][i] != places[1][i]]
    if len(moved) != 1:
        return 1
    inner = len({place[moved[0]] for place in places})
    return inner if count % (4 * inner) == 0 else 1


def kernel(
    outer, inner, heads,
    q_hbm, k_hbm, v_hbm, id_hbm, out_ref,
    q_ref, k_ref, v_ref, id_ref, loaded, kv, qs, top, acc, probs, done, id_col,
    along_send, across_send, block_recv, out_send, out_recv,
):
    reach = outer // 2
    q_heads, rows, size = qs.shape
    kv_heads = kv.shape[2] // 2
    group = q_heads // kv_heads
    out_rows = out_ref.shape[0]
    pieces = 2 * kv_heads
    factor = size ** -0.5 * math.log2(math.e)

    me = lax.axis_index("ctx")
    a, b = me // inner, me % inner
    place = lax.axis_index("head")
    has_prev, has_next = a > 0, a < outer - 1

    def span(p):
        return pl.ds(0, rows + ID_ROWS) if p == 0 else pl.ds(0, rows)

    loads = [
        pltpu.make_async_copy(source, held, loaded.at[i])
        for i, (source, held) in enumerate(
            ((k_hbm, k_ref), (v_hbm, v_ref), (id_hbm, id_ref), (q_hbm, q_ref))
        )
    ]
    for load in loads:
        load.start()

    barrier = pltpu.get_barrier_semaphore()

    def greet(device_id):
        pl.semaphore_signal(barrier, inc=1, device_id=device_id, device_id_type=MESH)

    @pl.when(has_prev)
    def _():
        greet({"ctx": me - inner})

    @pl.when(has_next)
    def _():
        greet({"ctx": me + inner})

    for step in range(1, inner):
        greet({"ctx": a * inner + (b + step) % inner})
    for step in range(1, heads):
        greet({"head": (place + step) % heads})

    def split_heads(ref, count, store):
        chunk = min(256, ref.shape[0])
        tokens = chunk // count
        row = lax.broadcasted_iota(jnp.int32, (chunk, chunk), 0)
        col = lax.broadcasted_iota(jnp.int32, (chunk, chunk), 1)
        order = jnp.where(col == (row % tokens) * count + row // tokens, 1.0, 0.0).astype(jnp.bfloat16)
        for i in range(ref.shape[0] // chunk):
            part = ref[i * chunk:(i + 1) * chunk, :]
            moved = jnp.dot(order, part, preferred_element_type=jnp.float32).astype(jnp.bfloat16)
            for h in range(count):
                store(h, pl.ds(i * tokens, tokens), moved[h * tokens:(h + 1) * tokens])

    def store_k(h, where, value):
        kv[0, b, 2 * h, where, :] = value

    def store_v(h, where, value):
        kv[0, b, 2 * h + 1, where, :] = value

    def store_q(h, where, value):
        qs[h, where, :] = value

    loads[0].wait()
    split_heads(k_ref, kv_heads, store_k)
    loads[1].wait()
    split_heads(v_ref, kv_heads, store_v)
    loads[2].wait()
    numbers = id_ref[...].astype(jnp.float32)
    line = lax.broadcasted_iota(jnp.int32, (ID_ROWS, size), 0)
    lines = jnp.zeros((ID_ROWS, size), jnp.float32)
    for i in range(rows // size):
        lines = jnp.where(line == i, numbers[i:i + 1, :], lines)
    kv[0, b, 0, rows:rows + ID_ROWS, :] = lines.astype(jnp.bfloat16)

    up, down = has_next.astype(jnp.int32), has_prev.astype(jnp.int32)
    greeted = up + down + (inner - 1) + (heads - 1)
    pl.semaphore_wait(barrier, greeted)

    def along(da, p):
        return pltpu.make_async_remote_copy(
            src_ref=kv.at[da, b, p, span(p)],
            dst_ref=kv.at[da + 1, b, p, span(p)],
            send_sem=along_send.at[da, p],
            recv_sem=block_recv.at[da + 1, b, p],
            device_id={"ctx": me + inner},
            device_id_type=MESH,
        )

    def across(da, p, to):
        return pltpu.make_async_remote_copy(
            src_ref=kv.at[da, b, p, span(p)],
            dst_ref=kv.at[da, b, p, span(p)],
            send_sem=across_send.at[da, to, p],
            recv_sem=block_recv.at[da, b, p],
            device_id={"ctx": a * inner + to},
            device_id_type=MESH,
        )

    def landed(da, at, p):
        return pltpu.make_async_remote_copy(
            src_ref=kv.at[da, at, p, span(p)],
            dst_ref=kv.at[da, at, p, span(p)],
            send_sem=along_send.at[0, p],
            recv_sem=block_recv.at[da, at, p],
            device_id={"ctx": me},
            device_id_type=MESH,
        )

    def needed(da, src, dst):
        if da == 0:
            return src < dst
        if da == reach:
            return src > dst
        return src != dst

    def spread(da, p, act):
        if da < reach:
            @pl.when(has_next)
            def _():
                act(along(da, p))
        for step in range(1, inner):
            to = (b + step) % inner

            @pl.when(needed(da, b, to))
            def _():
                act(across(da, p, to))

    for p in range(pieces):
        spread(0, p, lambda copy: copy.start())

    loads[3].wait()
    split_heads(q_ref, q_heads, store_q)

    row = lax.broadcasted_iota(jnp.int32, (rows, rows), 0)
    col = lax.broadcasted_iota(jnp.int32, (rows, rows), 1)

    def key_ids(da, at):
        held = kv[da, at, 0, rows:rows + ID_ROWS, :].astype(jnp.float32)
        return jnp.concatenate([held[i:i + 1, :] for i in range(rows // size)], axis=1)

    own_ids = key_ids(0, b)
    column = jnp.sum(jnp.where(row == col, own_ids, 0.0), axis=1, keepdims=True)
    id_col[...] = jnp.broadcast_to(column, id_col.shape)

    def wide(value, width):
        return jnp.concatenate([value] * (width // value.shape[1]), axis=1)

    def attend(da, at, g, first=False):
        same = wide(id_col[...], rows) == key_ids(da, at)
        if first:
            same = same & (col <= row)
        bias = jnp.where(same, 0.0, HIDDEN)
        keys = kv[da, at, 2 * g, :rows, :]
        values = kv[da, at, 2 * g + 1, :rows, :]
        values = jnp.concatenate([values, jnp.ones_like(values)], axis=1)
        for j in range(group):
            h = g * group + j
            scores = lax.dot_general(
                qs[h], keys, (((1,), (1,)), ((), ())), preferred_element_type=jnp.float32
            ) + bias
            highest = jnp.broadcast_to(jnp.max(scores, axis=1, keepdims=True), (rows, size))
            if not first:
                old = top[h]
                highest = jnp.maximum(old, highest)
            weights = jnp.exp2((scores - wide(highest, rows)) * factor).astype(jnp.bfloat16)
            product = jnp.dot(weights, values, preferred_element_type=jnp.float32)
            if not first:
                product = acc[h] * wide(jnp.exp2((old - highest) * factor), 2 * size) + product
            top[h] = highest
            acc[h] = product

    def attend_last(da, at, g):
        landed(da, at, 2 * g).wait_recv()
        bias = jnp.where(wide(id_col[...], rows) == key_ids(da, at), 0.0, HIDDEN)
        keys = kv[da, at, 2 * g, :rows, :]
        for j in range(group):
            h = g * group + j
            scores = lax.dot_general(
                qs[h], keys, (((1,), (1,)), ((), ())), preferred_element_type=jnp.float32
            ) + bias
            old = top[h]
            highest = jnp.maximum(
                old, jnp.broadcast_to(jnp.max(scores, axis=1, keepdims=True), (rows, size))
            )
            probs[j] = jnp.exp2((scores - wide(highest, rows)) * factor).astype(jnp.bfloat16)
            top[h] = jnp.exp2((old - highest) * factor)
        landed(da, at, 2 * g + 1).wait_recv()
        values = kv[da, at, 2 * g + 1, :rows, :]
        values = jnp.concatenate([values, jnp.ones_like(values)], axis=1)
        for j in range(group):
            h = g * group + j
            product = jnp.dot(probs[j], values, preferred_element_type=jnp.float32)
            close(h, acc[h] * wide(top[h], 2 * size) + product)
        keep(g)

    def pass_on(da, *which):
        @pl.when(a >= da)
        def _():
            for p in which:
                landed(da, b, p).wait_recv()
                spread(da, p, lambda copy: copy.start())

    def column_block(da, g):
        @pl.when(a >= da)
        def _():
            attend(da, b, g)

    def inner_blocks(da, g, last=False):
        if last:
            steps = inner - 1
        else:
            steps = inner
        if inner == 1:
            return

        def one(step, carry):
            at = (b + step) % inner

            @pl.when((a >= da) & needed(da, at, b))
            def _():
                for p in (2 * g, 2 * g + 1):
                    landed(da, at, p).wait_recv()
                attend(da, at, g)

            return carry

        if steps > 1:
            lax.fori_loop(1, steps, one, 0)
        if last:
            @pl.when(a >= da)
            def _():
                attend_last(da, (b + inner - 1) % inner, g)

            @pl.when(a < da)
            def _():
                finish(g)

    def give(h, to):
        return pltpu.make_async_remote_copy(
            src_ref=done.at[h, pl.ds(to * out_rows, out_rows)],
            dst_ref=out_ref.at[:, pl.ds(pl.multiple_of((place * q_heads + h) * size, size), size)],
            send_sem=out_send.at[h, to],
            recv_sem=out_recv.at[h, place],
            device_id={"head": to},
            device_id_type=MESH,
        )

    def taken(h, source):
        return pltpu.make_async_remote_copy(
            src_ref=done.at[h, pl.ds(0, out_rows)],
            dst_ref=out_ref.at[:, pl.ds(pl.multiple_of((source * q_heads + h) * size, size), size)],
            send_sem=out_send.at[h, source],
            recv_sem=out_recv.at[h, source],
            device_id={"head": source},
            device_id_type=MESH,
        )

    def close(h, total):
        done[h] = (total[:, :size] / total[:, size:]).astype(jnp.bfloat16)
        for step in range(1, heads):
            give(h, (place + step) % heads).start()

    def keep(g):
        for j in range(group):
            h = g * group + j
            out_ref[:, pl.ds(pl.multiple_of((place * q_heads + h) * size, size), size)] = done[
                h, pl.ds(pl.multiple_of(place * out_rows, out_rows), out_rows), :
            ]

    def finish(g):
        for j in range(group):
            close(g * group + j, acc[g * group + j])
        keep(g)

    groups = range(kv_heads)
    for g in groups:
        attend(0, b, g, first=True)
    def enter(g):
        pass_on(1, 2 * g, 2 * g + 1)
        column_block(1, g)

    enter(0)
    for g in groups:
        inner_blocks(0, g)
        for da in range(2, reach + 1):
            @pl.when(b > 0)
            def _():
                pass_on(da, 2 * g, 2 * g + 1)
                column_block(da, g)
                if da < reach:
                    inner_blocks(da - 1, g)

            @pl.when(b == 0)
            def _():
                inner_blocks(da - 1, g)
                pass_on(da, 2 * g, 2 * g + 1)
                column_block(da, g)

        if g + 1 < kv_heads:
            enter(g + 1)
        if inner > 1:
            @pl.when(b > 0)
            def _():
                inner_blocks(reach, g)
                inner_blocks(reach - 1, g, last=True)

            @pl.when(b == 0)
            def _():
                inner_blocks(reach, g, last=True)
        else:
            finish(g)

    for h in range(q_heads):
        for step in range(1, heads):
            taken(h, (place + step) % heads).wait_recv()
    for da in range(reach + 1):
        @pl.when(a >= da)
        def _():
            for p in range(pieces):
                spread(da, p, lambda copy: copy.wait_send())
    for h in range(q_heads):
        for step in range(1, heads):
            give(h, (place + step) % heads).wait_send()


def in_hbm(array):
    return pltpu.with_memory_space_constraint(array, pltpu.HBM)


def local(outer, inner, heads, queries, keys, values, doc_ids):
    rows, q_heads, size = queries.shape
    kv_heads = keys.shape[1]
    reach = outer // 2
    return pl.pallas_call(
        functools.partial(kernel, outer, inner, heads),
        out_shape=jax.ShapeDtypeStruct((rows // heads, heads * q_heads * size), jnp.bfloat16),
        in_specs=[pl.BlockSpec(memory_space=pltpu.HBM)] * 4,
        out_specs=pl.BlockSpec(memory_space=pltpu.VMEM),
        scratch_shapes=[
            pltpu.VMEM((rows * q_heads, size), jnp.bfloat16),
            pltpu.VMEM((rows * kv_heads, size), jnp.bfloat16),
            pltpu.VMEM((rows * kv_heads, size), jnp.bfloat16),
            pltpu.VMEM((rows // size, size), jnp.int32),
            pltpu.SemaphoreType.DMA((4,)),
            pltpu.VMEM((reach + 1, inner, 2 * kv_heads, rows + ID_ROWS, size), jnp.bfloat16),
            pltpu.VMEM((q_heads, rows, size), jnp.bfloat16),
            pltpu.VMEM((q_heads, rows, size), jnp.float32),
            pltpu.VMEM((q_heads, rows, 2 * size), jnp.float32),
            pltpu.VMEM((q_heads // kv_heads, rows, rows), jnp.bfloat16),
            pltpu.VMEM((q_heads, rows, size), jnp.bfloat16),
            pltpu.VMEM((rows, size), jnp.float32),
            pltpu.SemaphoreType.DMA((reach, 2 * kv_heads)),
            pltpu.SemaphoreType.DMA((reach + 1, inner, 2 * kv_heads)),
            pltpu.SemaphoreType.DMA((reach + 1, inner, 2 * kv_heads)),
            pltpu.SemaphoreType.DMA((q_heads, heads)),
            pltpu.SemaphoreType.DMA((q_heads, heads)),
        ],
        compiler_params=pltpu.CompilerParams(
            collective_id=0, has_side_effects=True, vmem_limit_bytes=48 * 1024 * 1024
        ),
    )(
        in_hbm(queries.reshape(rows * q_heads, size)),
        in_hbm(keys.reshape(rows * kv_heads, size)),
        in_hbm(values.reshape(rows * kv_heads, size)),
        in_hbm(doc_ids.reshape(rows // size, size)),
    )


def solution(mesh):
    inner = inner_size(mesh)
    return jax.shard_map(
        functools.partial(local, mesh.shape["ctx"] // inner, inner, mesh.shape["head"]),
        mesh=mesh,
        in_specs=(P("ctx", "head", None), P("ctx", "head", None), P("ctx", "head", None), P("ctx")),
        out_specs=P(("ctx", "head"), None),
        check_vma=False,
    )
```
